256 devices in a mesh: group: 4 (over z_lo), tensor: 64 (over x, y, z_hi, core).
Axes of the slice: x: 4, y: 4, z: 8 (z_hi: 2, z_lo: 4; z = z_hi * 4 + z_lo), core: 2. Of those that a mesh axis runs over, the one named last changes fastest.
Arguments:
- query_init: bfloat16 [5120, 8192], P(('group', 'tensor'))
- query_first: bfloat16 [5120, 8192], P(('group', 'tensor')), as said below
- query_second: bfloat16 [5120, 8192], P(('group', 'tensor'))
- key_init: bfloat16 [5120, 1024], P(('group', 'tensor'))
- key_first: bfloat16 [5120, 1024], P(('group', 'tensor'))
- key_second: bfloat16 [5120, 1024], P(('group', 'tensor'))
- value_init: bfloat16 [5120, 1024], P(('group', 'tensor'))
- value_first: bfloat16 [5120, 1024], P(('group', 'tensor'))
- value_second: bfloat16 [5120, 1024], P(('group', 'tensor'))
- output_init: bfloat16 [8192, 5120], P(('group', 'tensor'))
- output_first: bfloat16 [8192, 5120], P(('group', 'tensor'))
- output_second: bfloat16 [8192, 5120], P(('group', 'tensor'))
- hidden_rows: bfloat16 [16, 5120], P('group'), may hold values from -6 to 6
- cache_keys: bfloat16 [16, 8, 4096, 128], P('group', None, 'tensor'), may hold values from -256 to 256, as said below
- cache_values: bfloat16 [16, 8, 4096, 128], P('group', None, 'tensor'), may hold values from -6 to 6
- positions: int32 [16], P('group'), may hold values from 4096 to 8191
- lengths: int32 [16], P('group'), may hold values from 1 to 4096, as said below
Outputs:
- attended: bfloat16 [16, 5120], P('group')
The draws below stay inside these ranges and needn't reach their ends.
Inputs may be any that keep to these rules, and one draw needn't show every extreme that they name: `query_first`: each of the three arrays of a projection has the same shape; the policies differ from the initialization by task vectors of full rank. `cache_keys`: cached keys are real-valued and bounded. `lengths`: some row has exactly 4096 filled slots.
All inputs are finite; a program needn't handle non-finite values.
Results may differ from the reference program's by a relative error of at most 0.012.
The reference program's roundings to bfloat16 on the way count: a program that leaves them out, or rounds other values in their place, can miss the bound.
Values may be sent and summed in bfloat16 or wider, within the bound.
A program may use at most 64 MiB of HBM per device.

```python
import math
import jax
import jax.numpy as jnp
from jax import lax

D = 5120
HQ = 64
KVH = 8
HD = 128
LEN = 4096
ROWS = 16
POS_DEV = 64
N_TENSOR = 64


def task_matrices(key, salt, rows, cols, center):
    key = jax.random.fold_in(key, salt)
    keys = jax.random.split(key, 6)
    init = jax.random.normal(keys[0], (rows, cols), jnp.float32) / math.sqrt(rows)
    place = jnp.arange(rows, dtype=jnp.float32) / rows
    row_scale = jnp.exp(jax.random.uniform(keys[1], (rows, 1), jnp.float32) * math.log(10.0)) * jnp.exp(place * math.log(3.0))[:, None]
    col_scale = jnp.exp(jax.random.uniform(keys[2], (1, cols), jnp.float32) * math.log(10.0))
    phase = jax.random.uniform(keys[3], (), jnp.float32, 0.0, 2.0 * math.pi)
    share = center + 0.4 * jnp.sin(phase + 2.0 * math.pi * place)[:, None]
    common = jax.random.normal(keys[4], (rows, cols), jnp.float32)
    other = jax.random.normal(keys[5], (rows, cols), jnp.float32)
    size = 0.02 / math.sqrt(rows) * row_scale * col_scale
    first = init + size * common
    second = init + size * (share * common + jnp.sqrt(1.0 - share * share) * other)
    return (init, first, second)


def draw_query_init(key, part):
    center = 0.05
    return task_matrices(key, 11, D, HQ * HD, center)[0].astype(jnp.bfloat16)


def draw_query_first(key, part):
    center = 0.05
    return task_matrices(key, 11, D, HQ * HD, center)[1].astype(jnp.bfloat16)


def draw_query_second(key, part):
    center = 0.05
    return task_matrices(key, 11, D, HQ * HD, center)[2].astype(jnp.bfloat16)


def draw_key_init(key, part):
    center = 0.05
    return task_matrices(key, 12, D, KVH * HD, center)[0].astype(jnp.bfloat16)


def draw_key_first(key, part):
    center = 0.05
    return task_matrices(key, 12, D, KVH * HD, center)[1].astype(jnp.bfloat16)


def draw_key_second(key, part):
    center = 0.05
    return task_matrices(key, 12, D, KVH * HD, center)[2].astype(jnp.bfloat16)


def draw_value_init(key, part):
    center = 0.05
    return task_matrices(key, 13, D, KVH * HD, center)[0].astype(jnp.bfloat16)


def draw_value_first(key, part):
    center = 0.05
    return task_matrices(key, 13, D, KVH * HD, center)[1].astype(jnp.bfloat16)


def draw_value_second(key, part):
    center = 0.05
    return task_matrices(key, 13, D, KVH * HD, center)[2].astype(jnp.bfloat16)


def draw_output_init(key, part):
    center = 0.05
    return task_matrices(key, 14, HQ * HD, D, center)[0].astype(jnp.bfloat16)


def draw_output_first(key, part):
    center = 0.05
    return task_matrices(key, 14, HQ * HD, D, center)[1].astype(jnp.bfloat16)


def draw_output_second(key, part):
    center = 0.05
    return task_matrices(key, 14, HQ * HD, D, center)[2].astype(jnp.bfloat16)


def draw_cache_keys(key, part):
    key = jax.random.fold_in(key, 41)
    keys = jax.random.split(key, 1)
    base = jax.random.normal(keys[0], (ROWS, KVH, LEN, HD), jnp.float32)
    base = jnp.clip(base, -6.0, 6.0)
    return jnp.clip(base, -256.0, 256.0).astype(jnp.bfloat16)


def draw_lengths(key, part):
    key = jax.random.fold_in(key, 53)
    keys = jax.random.split(key, 5)
    levels = LEN.bit_length() - 1
    exponent = jax.random.randint(keys[0], (ROWS,), 0, levels + 1)
    lowest = jnp.left_shift(jnp.ones((ROWS,), jnp.int32), exponent.astype(jnp.int32))
    extra = jax.random.randint(keys[1], (ROWS,), 0, lowest)
    drawn = jnp.minimum(lowest + extra, LEN)
    full_row = jax.random.randint(keys[2], (), 0, ROWS)
    short_row = (full_row + 1 + jax.random.randint(keys[3], (), 0, ROWS - 1)) % ROWS
    short_length = jax.random.randint(keys[4], (), 1, 5)
    places = jnp.arange(ROWS)
    result = jnp.where(places == full_row, LEN, drawn)
    result = jnp.where(places == short_row, short_length, result)
    return result.astype(jnp.int32)


def touch_ends(entries, key, least, top_value):
    longest = entries.shape.index(max(entries.shape))
    spots = []
    for shift in (0, 1):
        where = [jax.random.randint(jax.random.fold_in(key, axis), (), 0, length) for axis, length in enumerate(entries.shape)]
        where[longest] = (where[longest] + shift) % entries.shape[longest]
        spots.append(tuple(where))
    return entries.at[spots[0]].set(least).at[spots[1]].set(top_value)


def block_levels(rng, dims, shards, low, largest):
    level = 1.0
    for position, blocks in shards:
        heights = jax.random.uniform(jax.random.fold_in(jax.random.fold_in(rng, 6), position), (blocks,), jnp.float32, low / len(shards), largest / len(shards))
        level = level * jnp.repeat(jnp.exp(heights), dims[position] // blocks).reshape((-1,) + (1,) * (len(dims) - 1 - position))
    return level


def noise(rng, extent, deviation, reach, cuts=(), kind=jnp.bfloat16):
    values = jax.random.normal(rng, extent, jnp.float32) * deviation
    if len(cuts) > 0:
        values = block_levels(rng, extent, cuts, -0.22, 0.18) * values
    return jnp.clip(values, min=-reach, max=reach).astype(kind)


def setup_inputs(seed: int = 0) -> dict:
    seeds = jax.random.split(jax.random.key(seed), 18)
    return {
        "query_init": draw_query_init(jax.random.fold_in(seeds[17], 71), 0),
        "query_first": draw_query_first(jax.random.fold_in(seeds[17], 71), 0),
        "query_second": draw_query_second(jax.random.fold_in(seeds[17], 71), 0),
        "key_init": draw_key_init(jax.random.fold_in(seeds[17], 71), 0),
        "key_first": draw_key_first(jax.random.fold_in(seeds[17], 71), 0),
        "key_second": draw_key_second(jax.random.fold_in(seeds[17], 71), 0),
        "value_init": draw_value_init(jax.random.fold_in(seeds[17], 71), 0),
        "value_first": draw_value_first(jax.random.fold_in(seeds[17], 71), 0),
        "value_second": draw_value_second(jax.random.fold_in(seeds[17], 71), 0),
        "output_init": draw_output_init(jax.random.fold_in(seeds[17], 71), 0),
        "output_first": draw_output_first(jax.random.fold_in(seeds[17], 71), 0),
        "output_second": draw_output_second(jax.random.fold_in(seeds[17], 71), 0),
        "hidden_rows": noise(seeds[12], (ROWS, D), 1.0, 6.0, ((0, 4),)),
        "cache_keys": draw_cache_keys(jax.random.fold_in(seeds[17], 71), 0),
        "cache_values": noise(seeds[14], (ROWS, KVH, LEN, HD), 1.0, 6.0, ((0, 4), (2, 64))),
        "positions": touch_ends(jax.random.randint(seeds[15], (ROWS,), LEN, 2 * LEN), jax.random.fold_in(seeds[15], 1), LEN, (2 * LEN) - 1).astype(jnp.int32),
        "lengths": draw_lengths(jax.random.fold_in(seeds[17], 71), 0),
    }


blend = 0.5
rope_base = 1000000.0

def rotate(values, positions):
    half = values.shape[-1] // 2
    steps = jnp.arange(half, dtype=jnp.float32) * (2.0 / values.shape[-1])
    freq = rope_base ** (-steps)
    angle = positions.astype(jnp.float32)[:, None] * freq[None, :]
    cosine = jnp.cos(angle)[:, None, :]
    sine = jnp.sin(angle)[:, None, :]
    first = values[..., :half]
    second = values[..., half:]
    return jnp.concatenate([first * cosine - second * sine, second * cosine + first * sine], axis=-1)

def merge_task(init, first, second):
    base = init.astype(jnp.float32)
    delta_a = first.astype(jnp.float32) - base
    delta_b = second.astype(jnp.float32) - base
    total_aa = jnp.sum(delta_a * delta_a)
    total_bb = jnp.sum(delta_b * delta_b)
    total_ab = jnp.sum(delta_a * delta_b)
    cosine = total_ab / jnp.sqrt(total_aa * total_bb + 1e-06)
    angle = jnp.arccos(cosine)
    inverse = 1.0 / jnp.sin(angle)
    merged = base + jnp.sin((1.0 - blend) * angle) * inverse * delta_a + jnp.sin(blend * angle) * inverse * delta_b
    return merged.astype(jnp.bfloat16)

def reference(query_init, query_first, query_second, key_init, key_first, key_second, value_init, value_first, value_second, output_init, output_first, output_second, hidden_rows, cache_keys, cache_values, positions, lengths):
    query_merged = merge_task(query_init, query_first, query_second)
    key_merged = merge_task(key_init, key_first, key_second)
    value_merged = merge_task(value_init, value_first, value_second)
    output_merged = merge_task(output_init, output_first, output_second)
    scale = 1.0 / math.sqrt(HD)
    query = jnp.dot(hidden_rows, query_merged, preferred_element_type=jnp.float32).reshape(ROWS, HQ, HD)
    query = rotate(query, positions).astype(jnp.bfloat16)
    new_key = jnp.dot(hidden_rows, key_merged, preferred_element_type=jnp.float32).reshape(ROWS, KVH, HD)
    new_key = rotate(new_key, positions).astype(jnp.bfloat16)
    new_value = jnp.dot(hidden_rows, value_merged, preferred_element_type=jnp.float32).astype(jnp.bfloat16).reshape(ROWS, KVH, HD)

    def one_row(items):
        row_query, keys, values, row_key, row_value, length = items
        grouped = row_query.reshape(KVH, HQ // KVH, HD).astype(jnp.float32)
        scores = jnp.einsum('kgd,kpd->kgp', grouped, keys.astype(jnp.float32)) * scale
        valid = (jnp.arange(LEN, dtype=jnp.int32) < length)[None, None, :]
        valid = jnp.broadcast_to(valid, scores.shape).reshape(KVH, HQ // KVH, N_TENSOR, POS_DEV)
        blocked = scores.reshape(KVH, HQ // KVH, N_TENSOR, POS_DEV)
        peaks = lax.optimization_barrier(jnp.max(jnp.where(valid, blocked, -1e+30), axis=-1))
        weights = jnp.where(valid, jnp.exp(blocked - peaks[..., None]), 0.0).astype(jnp.bfloat16)
        totals = lax.optimization_barrier(jnp.sum(weights.astype(jnp.float32), axis=-1))
        blocked_values = values.astype(jnp.float32).reshape(KVH, N_TENSOR, POS_DEV, HD)
        mixes = jnp.einsum('kgbp,kbpd->kgbd', weights.astype(jnp.float32), blocked_values)
        peak = lax.optimization_barrier(jnp.max(peaks, axis=-1))
        factor = jnp.exp(peaks - peak[..., None])
        total = lax.optimization_barrier(jnp.sum(totals * factor, axis=-1))
        mixed = lax.optimization_barrier(jnp.sum(mixes * factor[..., None], axis=2))
        own = jnp.einsum('kgd,kd->kg', grouped, row_key.astype(jnp.float32)) * scale
        top = jnp.maximum(peak, own)
        old_factor = jnp.exp(peak - top)
        own_factor = jnp.exp(own - top)
        denom = total * old_factor + own_factor
        heads = (mixed * old_factor[..., None] + own_factor[..., None] * row_value.astype(jnp.float32)[:, None, :]) / denom[..., None]
        return heads.astype(jnp.bfloat16).reshape(HQ * HD)
    heads = lax.map(one_row, (query, cache_keys, cache_values, new_key, new_value, lengths))
    return jnp.dot(heads, output_merged, preferred_element_type=jnp.float32).astype(jnp.bfloat16)
```

```python
import math

import jax
import jax.numpy as jnp
import numpy as np
from jax import lax
from jax.experimental import pallas as pl
from jax.experimental.pallas import tpu as pltpu
from jax.sharding import PartitionSpec as P

MESH = pl.DeviceIdType.MESH
F32 = jnp.float32
BF16 = jnp.bfloat16
G, XY, W = 4, 16, 4
R, HD, SPAN = 4, 128, 64
QW, KW, OW = 8192, 1024, 5120
DEPTH, ODEPTH = 20, 32
SCALE = 1.0 / math.sqrt(HD)


def kernel(
    qi, qf, qs, ki, kf, ks, vi, vf, vs, oi, of, os_, hid, ck, cv, pos, lens, freq,
    out,
    wq, wk, wv, wo, pq, pk, pv, po, kc, vc, hv,
    hsend, hrecv, hfull, sa, ra, sb, rb, mq, mkv, mo,
    qsend, qrecv, zsend, zrecv, slab, qb, qk,
    asend, arecv, xsend, xrecv, hd, bsend, brecv, ysend, yrecv, osend, obuf,
    load_sem, swap_send, swap_recv, send_sem, recv_sem,
):
    g = lax.axis_index("group")
    t = lax.axis_index("tensor")
    xy, w = t // 4, t % 4
    zh, c = w // 2, w % 2
    x = xy // 4
    z = zh * 4 + g

    def remote(src, dst, stage, device):
        return pltpu.make_async_remote_copy(
            src_ref=src, dst_ref=dst, send_sem=send_sem.at[stage], recv_sem=recv_sem.at[stage],
            device_id=device, device_id_type=MESH,
        )

    def settle(ref, sem):
        pltpu.make_async_copy(ref, ref, sem).wait()

    raw = [(qi, qf, qs), (ki, kf, ks), (vi, vf, vs), (oi, of, os_)]
    mine = [wq, wk, wv, wo]
    theirs = [pq, pk, pv, po]
    loads = []
    for m in range(4):
        for j in range(3):
            loads.append(pltpu.make_async_copy(raw[m][j], mine[m].at[j], load_sem.at[3 * m + j]))
    loads.append(pltpu.make_async_copy(ck, kc, load_sem.at[12]))
    loads.append(pltpu.make_async_copy(cv, vc, load_sem.at[13]))
    loads.append(pltpu.make_async_copy(hid, hv, load_sem.at[14]))
    for copy in loads:
        copy.start()

    def plane(i):
        place = (xy * 2 + c + i) % 32
        return (g, (place // 2) * 4 + zh * 2 + place % 2)

    def column(i):
        place = (g * 4 + w + i) % 16
        return (place // 4, xy * 4 + place % 4)

    barrier = pltpu.get_barrier_semaphore()

    def greet_plane(i, _):
        pl.semaphore_signal(barrier, inc=1, device_id=plane(i), device_id_type=MESH)
        return 0

    def greet_column(i, _):
        place = (g * 4 + w + i) % 16
        there = (place // 4, xy * 4 + place % 4)
        chip = (place // 4 == g) & ((place % 4) // 2 == zh)

        @pl.when(jnp.logical_not(chip))
        def _():
            pl.semaphore_signal(barrier, inc=1, device_id=there, device_id_type=MESH)

        return 0

    lax.fori_loop(1, 32, greet_plane, 0)
    lax.fori_loop(1, 16, greet_column, 0)
    pl.semaphore_wait(barrier, 45)

    other = (g, t + 1 - 2 * c)
    swaps = []
    for m, width in enumerate((QW // 2, KW // 2, KW // 2, OW // 2)):
        for j in range(3):
            start = pl.multiple_of((1 - c) * width, 128)
            swaps.append(
                pltpu.make_async_remote_copy(
                    src_ref=raw[m][j].at[:, pl.ds(start, width)], dst_ref=theirs[m].at[j],
                    send_sem=swap_send.at[3 * m + j], recv_sem=swap_recv.at[3 * m + j],
                    device_id=other, device_id_type=MESH,
                )
            )
    for copy in swaps:
        copy.start()

    loads[14].wait()
    place = 40 * (t // 2)
    base = jnp.minimum(place // 128, 8) * 128
    lane = lax.broadcasted_iota(jnp.int32, (256, 128), 1)
    row = lax.broadcasted_iota(jnp.int32, (256, 128), 0)
    piece, step = lane // 32, lane % 32
    wanted = place - base + step + 20 * jnp.where(piece == 0, c, 1 - c)
    pick = jnp.where((row == wanted) & (lane < 64) & (step < 20), 1.0, 0.0).astype(BF16)
    for to in range(G):
        window = hv[:, pl.ds(pl.multiple_of(1280 * to + base, 128), 256)]
        hsend[to] = jnp.dot(window, pick, preferred_element_type=F32)
    for i in range(1, G):
        to = (g + i) % G
        remote(hsend.at[to], hrecv.at[g], 0, (to, t)).start()
    hrecv[g] = hsend[g]

    def sums(ref, rows, width, step):
        def body(i, acc):
            at = pl.ds(pl.multiple_of(i * step, step), step)
            init = ref[0, :, at].astype(F32)
            a = ref[1, :, at].astype(F32) - init
            b = ref[2, :, at].astype(F32) - init
            return (acc[0] + a * a, acc[1] + b * b, acc[2] + a * b)

        zero = jnp.zeros((rows, step), F32)
        totals = lax.fori_loop(0, width // step, body, (zero, zero, zero), unroll=2)
        done = []
        for total in totals:
            line = jnp.sum(total, axis=0, keepdims=True)
            done.append(sum(line[:, 128 * j : 128 * (j + 1)] for j in range(step // 128)))
        return done

    sub16 = lax.broadcasted_iota(jnp.int32, (16, 128), 0)
    lane16 = lax.broadcasted_iota(jnp.int32, (16, 128), 1)
    stack = jnp.zeros((16, 128), F32)
    for m, (ref, rows, width) in enumerate(
        ((wq, DEPTH, QW), (wk, DEPTH, KW), (wv, DEPTH, KW), (wo, ODEPTH, OW))
    ):
        for j in range(3):
            loads[3 * m + j].wait()
        for kind, line in enumerate(sums(ref, rows, width, 256)):
            stack = jnp.where(sub16 == 4 * kind + m, line, stack)
    stack = jnp.sum(stack, axis=1, keepdims=True)
    sa[...] = jnp.sum(jnp.where(sub16 == lane16, stack, 0.0), axis=0, keepdims=True)

    def to_plane(src, dst, stage):
        def body(i, _):
            there = (xy + i) % XY
            remote(src(there), dst, stage, (g, there * 4 + w)).start()
            return 0

        lax.fori_loop(1, XY, body, 0)

    to_plane(lambda there: sa, ra.at[xy], 1)
    ra[xy] = sa[...]
    settle(ra.at[pl.ds(0, XY - 1)], recv_sem.at[1])
    sb[...] = jnp.sum(ra[...], axis=0)

    def send_sums(i, _):
        remote(sb, rb.at[g * 4 + w], 2, column(i)).start()
        return 0

    lax.fori_loop(1, 16, send_sums, 0)
    rb[g * 4 + w] = sb[...]

    mq[...] = jnp.zeros_like(mq)
    mkv[...] = jnp.zeros_like(mkv)
    settle(hrecv.at[pl.ds(0, G - 1)], recv_sem.at[0])
    for i in range(G):
        hfull[4 * i : 4 * i + 4, :] = hrecv[i]
    rows_all = hfull[...].astype(BF16)[:, :64]
    angle_row = lax.broadcasted_iota(jnp.int32, (R, HD), 0)
    at = jnp.zeros((R, HD), F32)
    length = jnp.zeros((32, 256), jnp.int32)
    row32 = lax.broadcasted_iota(jnp.int32, (32, 256), 0) % R
    for r in range(R):
        at = jnp.where(angle_row == r, pos[r].astype(F32), at)
        length = jnp.where(row32 == r, lens[r], length)
    angle = at * freq[...]
    half = lax.broadcasted_iota(jnp.int32, (R, HD), 1) < HD // 2
    cosine = jnp.cos(angle)
    sine = jnp.sin(angle)
    sine = jnp.where(half, -sine, sine)

    def rotate(value):
        return value * cosine + pltpu.roll(value, HD // 2, 1) * sine

    for copy in swaps:
        copy.wait_recv()
    settle(rb.at[pl.ds(0, 15)], recv_sem.at[2])
    total = jnp.broadcast_to(jnp.sum(rb[...], axis=0), (8, 128))
    bb = pltpu.roll(total, 124, 1)
    ab = pltpu.roll(total, 120, 1)
    similar = ab / jnp.sqrt(total * bb + 1e-06)
    share = 1.0 / jnp.sqrt(2.0 * (1.0 + similar))
    lane8 = lax.broadcasted_iota(jnp.int32, (8, 128), 1)
    shares = [
        jnp.sum(jnp.where(lane8 == m, share, 0.0), axis=1, keepdims=True)[0:1] for m in range(4)
    ]

    def merge(init, first, second, factor):
        base = init.astype(F32)
        a = first.astype(F32) - base
        b = second.astype(F32) - base
        return (base + factor * a + factor * b).astype(BF16)

    def merge_into(dst, rows, offset, own, swapped, own_row, other_row, width, factor, step):
        def body(i, _):
            there = pl.ds(pl.multiple_of(i * step, step), step)
            here = pl.ds(pl.multiple_of(c * width + i * step, step), step)
            to = pl.ds(pl.multiple_of(offset + i * step, step), step)
            dst[own_row, to] = merge(own[0, :, here], own[1, :, here], own[2, :, here], factor)
            dst[other_row, to] = merge(
                swapped[0, :, there], swapped[1, :, there], swapped[2, :, there], factor
            )
            return 0

        lax.fori_loop(0, width // step, body, 0, unroll=2)

    top, bottom = pl.ds(0, DEPTH), pl.ds(32, DEPTH)
    merge_into(mq, DEPTH, 0, wq, pq, top, bottom, QW // 2, shares[0], 256)
    merge_into(mkv, DEPTH, 0, wk, pk, top, bottom, KW // 2, shares[1], 256)
    merge_into(mkv, DEPTH, KW // 2, wv, pv, top, bottom, KW // 2, shares[2], 256)

    new = jnp.dot(rows_all, mkv[...], preferred_element_type=F32)
    for to in range(XY):
        for j in range(2):
            part = jnp.dot(
                rows_all, mq[:, 2048 * j + 128 * to : 2048 * j + 128 * (to + 1)],
                preferred_element_type=F32,
            )
            for i in range(G):
                qsend[to, 4 * j + i] = part[4 * i : 4 * i + 4]
        tile = new[:, 128 * (to // 2) : 128 * (to // 2 + 1)]
        for i in range(2):
            start = 8 * (to % 2) + 4 * i
            qsend[to, 8 + i] = tile[start : start + 4]
    to_plane(lambda there: qsend.at[there], qrecv.at[xy], 3)
    qrecv[xy] = qsend[xy]

    merge_into(
        mo, ODEPTH, 0, wo, po, pl.ds(pl.multiple_of(32 * c, 32), 32),
        pl.ds(pl.multiple_of(32 * (1 - c), 32), 32), OW // 2, shares[3], 256,
    )

    settle(qrecv.at[pl.ds(0, XY - 1)], recv_sem.at[3])
    total = jnp.sum(qrecv[...], axis=0)
    for i in range(G):
        zsend[i, 0] = total[i]
        zsend[i, 1] = total[4 + i]
        zsend[i, 2] = total[8 + i % 2]

    def to_z(src, dst, stage):
        def body(i, _):
            there = (z + i) % 8
            group = there % 4
            remote(src(group), dst, stage, (group, xy * 4 + (there // 4) * 2 + c)).start()
            return 0

        lax.fori_loop(1, 8, body, 0)

    to_z(lambda group: zsend.at[group], zrecv.at[z], 4)
    zrecv[z] = zsend[g]
    settle(zrecv.at[pl.ds(0, 7)], recv_sem.at[4])
    total = jnp.sum(zrecv[...], axis=0)
    rounded = lambda value: value.astype(BF16).astype(F32)
    slab[0] = rounded(rotate(total[0]))
    slab[1] = rounded(rotate(total[1]))
    slab[2] = rounded(jnp.where(xy < 8, rotate(total[2]), total[2]))

    def to_everyone(src, dst, stage):
        def body(i, _):
            remote(src, dst, stage, plane(i)).start()
            return 0

        lax.fori_loop(1, 32, body, 0)

    to_everyone(slab, qb.at[c * 16 + xy], 5)
    qb[c * 16 + xy] = slab[...]
    loads[12].wait()
    loads[13].wait()
    settle(qb.at[pl.ds(0, 31)], recv_sem.at[5])

    lane = lax.broadcasted_iota(jnp.int32, (32, 256), 1)
    valid = (lane // SPAN == row32) & (t * SPAN + lane % SPAN < length)
    lane32 = lax.broadcasted_iota(jnp.int32, (32, 128), 1)
    for high in range(2):
        stats = jnp.zeros((32, 128), F32)
        for gamma in range(4):
            half_c, j = gamma // 2, gamma % 2
            k = 2 * gamma + high
            for i in range(8):
                qk[k, 4 * i : 4 * i + 4, :] = qb[half_c * 16 + 8 * high + i, j]
            keys = kc[:, k].reshape(R * SPAN, HD)
            values = vc[:, k].reshape(R * SPAN, HD)
            score = lax.dot_general(
                qk[k].astype(BF16), keys, (((1,), (1,)), ((), ())), preferred_element_type=F32
            )
            score = jnp.where(valid, score * SCALE, -1e30)
            peak = jnp.max(score, axis=1, keepdims=True)
            weight = jnp.where(valid, jnp.exp(score - peak), 0.0).astype(BF16)
            mass = jnp.sum(weight.astype(F32), axis=1, keepdims=True)
            mixed = jnp.dot(weight, values, preferred_element_type=F32)
            for i in range(8):
                asend[8 * high + i, gamma] = mixed[4 * i : 4 * i + 4]
            stats = jnp.where(lane32 == gamma, peak, stats)
            stats = jnp.where(lane32 == 64 + gamma, mass, stats)
        for i in range(8):
            asend[8 * high + i, 4] = stats[4 * i : 4 * i + 4]
    to_plane(lambda there: asend.at[there], arecv.at[xy], 6)
    arecv[xy] = asend[xy]

    k = 2 * w + xy // 8
    query = qb[zh * 16 + xy, c]
    first = (k // 4) * 16 + 2 * (k % 4) + g // 2
    new_key = qb[first, 2]
    new_value = qb[first + 8, 2]
    own = jnp.sum(query * new_key, axis=1, keepdims=True) * SCALE

    settle(arecv.at[pl.ds(0, XY - 1)], recv_sem.at[6])
    stats = arecv[:, 4]
    peaks = jnp.max(stats, axis=0)
    factors = jnp.exp(stats - peaks)
    mass = jnp.zeros((R, HD), F32)
    for i in range(XY):
        mass = mass + factors[i] * pltpu.roll(stats[i], 64, 1)
    lane4 = lax.broadcasted_iota(jnp.int32, (R, HD), 1)
    for gamma in range(4):
        mixed = jnp.zeros((R, HD), F32)
        for i in range(XY):
            mixed = mixed + arecv[i, gamma] * factors[i][:, gamma : gamma + 1]
        peak = peaks[:, gamma : gamma + 1]
        here = w == gamma
        added = jnp.where(here, own, peak)
        most = jnp.maximum(peak, added)
        old = jnp.exp(peak - most)
        fresh = jnp.where(here, jnp.exp(added - most), 0.0)
        xsend[gamma, 0] = mixed * old + fresh * new_value
        xsend[gamma, 1] = jnp.where(lane4 < 64, most, mass[:, gamma : gamma + 1] * old + fresh)

    def send_heads(i, _):
        there = column(i)
        remote(xsend.at[there[0]], xrecv.at[g * 4 + w], 7, there).start()
        return 0

    lax.fori_loop(1, 16, send_heads, 0)
    xrecv[g * 4 + w] = xsend[g]
    settle(xrecv.at[pl.ds(0, 15)], recv_sem.at[7])
    for i in range(G):
        peak = [xrecv[4 * i + j, 1][:, 0:1] for j in range(W)]
        mass = [xrecv[4 * i + j, 1][:, 64:65] for j in range(W)]
        most = jnp.maximum(jnp.maximum(peak[0], peak[1]), jnp.maximum(peak[2], peak[3]))
        factor = [jnp.exp(p - most) for p in peak]
        bottom = sum(f * l for f, l in zip(factor, mass))
        top = sum(f * xrecv[4 * i + j, 0] for j, f in enumerate(factor))
        hd[4 * i : 4 * i + 4, :] = top / bottom
    heads = hd[...]
    heads = jnp.where(zh == 1, pltpu.roll(heads, 64, 1), heads).astype(BF16)[:, :64]

    for tile in range(20):
        part = jnp.dot(
            heads, mo[:, 128 * tile : 128 * (tile + 1)], preferred_element_type=F32
        )
        for i in range(G):
            if tile < XY:
                bsend[tile, i] = part[4 * i : 4 * i + 4]
            else:
                bsend[4 * i + tile - XY, 4] = part[4 * i : 4 * i + 4]
    to_plane(lambda there: bsend.at[there], brecv.at[xy], 8)
    brecv[xy] = bsend[xy]
    settle(brecv.at[pl.ds(0, XY - 1)], recv_sem.at[8])
    total = jnp.sum(brecv[...], axis=0)
    for i in range(G):
        ysend[i, 0] = total[i]
        ysend[i, 1] = total[4]
    to_z(lambda group: ysend.at[group], yrecv.at[z], 9)
    yrecv[z] = ysend[g]
    settle(yrecv.at[pl.ds(0, 7)], recv_sem.at[9])
    osend[...] = jnp.sum(yrecv[...], axis=0)
    to_everyone(osend, obuf.at[c * 16 + xy], 10)
    obuf[c * 16 + xy] = osend[...]
    settle(obuf.at[pl.ds(0, 31)], recv_sem.at[10])
    for half_c in range(2):
        for tile in range(20):
            start = half_c * (OW // 2) + 128 * tile
            if tile < XY:
                value = obuf[half_c * 16 + tile, 0]
            else:
                value = obuf[half_c * 16 + 4 * g + tile - XY, 1]
            out[:, start : start + 128] = value.astype(out.dtype)

    for copy in swaps:
        copy.wait_send()
    for stage, ref, count in (
        (0, hrecv, 3), (1, ra, 15), (2, rb, 15), (3, qrecv, 15), (4, zrecv, 7), (5, qb, 31),
        (6, arecv, 15), (7, xrecv, 15), (8, brecv, 15), (9, yrecv, 7), (10, obuf, 31),
    ):
        settle(ref.at[pl.ds(0, count)], send_sem.at[stage])


def shards(*args):
    freq = 1000000.0 ** (-np.arange(HD // 2) / (HD // 2))
    freq = jnp.asarray(np.concatenate([freq, freq])[None, :], F32)
    any_, vmem, smem = (
        pl.BlockSpec(memory_space=space) for space in (pl.ANY, pltpu.VMEM, pltpu.SMEM)
    )
    f32 = lambda *shape: pltpu.VMEM(shape, F32)
    bf16 = lambda *shape: pltpu.VMEM(shape, BF16)
    return pl.pallas_call(
        kernel,
        out_shape=jax.ShapeDtypeStruct((R, OW), BF16),
        in_specs=[any_] * 15 + [smem] * 2 + [vmem],
        out_specs=vmem,
        scratch_shapes=[
            bf16(3, DEPTH, QW), bf16(3, DEPTH, KW), bf16(3, DEPTH, KW), bf16(3, ODEPTH, OW),
            bf16(3, DEPTH, QW // 2), bf16(3, DEPTH, KW // 2), bf16(3, DEPTH, KW // 2), bf16(3, ODEPTH, OW // 2),
            bf16(R, 8, SPAN, HD), bf16(R, 8, SPAN, HD), bf16(R, 5120),
            f32(G, R, HD), f32(G, R, HD), f32(16, HD),
            f32(1, HD), f32(XY, 1, HD), f32(1, HD), f32(16, 1, HD),
            bf16(64, QW // 2), bf16(64, KW), bf16(64, OW // 2),
            f32(XY, 10, R, HD), f32(XY, 10, R, HD), f32(G, 3, R, HD), f32(8, 3, R, HD),
            f32(3, R, HD), f32(32, 3, R, HD), f32(8, 32, HD),
            f32(XY, 5, R, HD), f32(XY, 5, R, HD), f32(G, 2, R, HD), f32(16, 2, R, HD), f32(16, HD),
            f32(XY, 5, R, HD), f32(XY, 5, R, HD), f32(G, 2, R, HD), f32(8, 2, R, HD),
            f32(2, R, HD), f32(32, 2, R, HD),
            pltpu.SemaphoreType.DMA((15,)), pltpu.SemaphoreType.DMA((12,)), pltpu.SemaphoreType.DMA((12,)),
            pltpu.SemaphoreType.DMA((11,)), pltpu.SemaphoreType.DMA((11,)),
        ],
        compiler_params=pltpu.CompilerParams(
            collective_id=0, has_side_effects=True, vmem_limit_bytes=48 * 1024 * 1024
        ),
        cost_estimate=pl.CostEstimate(flops=40_000_000, bytes_accessed=4_000_000, transcendentals=100_000),
    )(*args, freq)


def solution(mesh):
    both = P(("group", "tensor"), None)
    cache = P("group", None, "tensor", None)
    in_specs = (both,) * 12 + (P("group", None), cache, cache, P("group"), P("group"))
    return jax.shard_map(
        shards, mesh=mesh, in_specs=in_specs, out_specs=P("group", None), check_vma=False
    )
```

```python
import math

import jax
import jax.numpy as jnp
import numpy as np
from jax import lax
from jax.experimental import pallas as pl
from jax.experimental.pallas import tpu as pltpu
from jax.sharding import PartitionSpec as P

MESH = pl.DeviceIdType.MESH
F32 = jnp.float32
BF16 = jnp.bfloat16
G, XY, W = 4, 16, 4
R, HD, SPAN = 4, 128, 64
QW, KW, OW = 8192, 1024, 5120
DEPTH, ODEPTH = 20, 32
FREQ = (1000000.0 ** (-np.arange(HD // 2) / (HD // 2))).astype(np.float32)
SCALE = 1.0 / math.sqrt(HD)


def kernel(
    qi, qf, qs, ki, kf, ks, vi, vf, vs, oi, of, os_, hid, ck, cv, pos_in, lens_in,
    out,
    pos, lens,
    wq, wk, wv, wo, pq, pk, pv, po, keys, values, hv,
    hsend, hrecv, hfull, sa, ra, sb, rb, mq, mkv, mo,
    qsend, qrecv, ksend, krecv, zsend, zrecv, nsend, nrecv,
    asend, arecv, hd, bsend, brecv, ysend, yrecv, osend, obuf,
    load_sem, swap_send, swap_recv, send_sem, recv_sem,
):
    g = lax.axis_index("group")
    t = lax.axis_index("tensor")
    xy, w = t // 4, t % 4
    zh, c = w // 2, w % 2
    x = xy // 4
    z = zh * 4 + g
    my_row = (xy % 8) // 2
    my_kind = 2 * (xy % 2) + xy // 8
    my_kv = 4 * c + my_kind

    def remote(src, dst, stage, device):
        return pltpu.make_async_remote_copy(
            src_ref=src, dst_ref=dst, send_sem=send_sem.at[stage], recv_sem=recv_sem.at[stage],
            device_id=device, device_id_type=MESH,
        )

    def settle(ref, sem):
        pltpu.make_async_copy(ref, ref, sem).wait()

    raw = [(qi, qf, qs), (ki, kf, ks), (vi, vf, vs), (oi, of, os_)]
    mine = [wq, wk, wv, wo]
    theirs = [pq, pk, pv, po]
    loads = []
    for m in range(4):
        for j in range(3):
            loads.append(pltpu.make_async_copy(raw[m][j], mine[m].at[j], load_sem.at[3 * m + j]))
    place = 2 * xy + c
    loads.append(pltpu.make_async_copy(ck.at[my_row, my_kv], keys.at[place], load_sem.at[12]))
    loads.append(pltpu.make_async_copy(cv.at[my_row, my_kv], values.at[place], load_sem.at[13]))
    loads.append(pltpu.make_async_copy(hid, hv, load_sem.at[14]))
    loads.append(pltpu.make_async_copy(pos_in, pos, load_sem.at[15]))
    loads.append(pltpu.make_async_copy(lens_in, lens, load_sem.at[16]))
    for copy in loads:
        copy.start()

    def plane(i):
        place = (xy * 2 + c + i) % 32
        return (g, (place // 2) * 4 + zh * 2 + place % 2)

    def column(i):
        place = (g * 4 + w + i) % 16
        return (place // 4, xy * 4 + place % 4)

    barrier = pltpu.get_barrier_semaphore()

    def greet(i, _):
        pl.semaphore_signal(barrier, inc=1, device_id=plane(i), device_id_type=MESH)
        return 0

    def greet_column(i, _):
        pl.semaphore_signal(barrier, inc=1, device_id=column(i), device_id_type=MESH)
        return 0

    lax.fori_loop(1, 16, greet_column, 0)
    lax.fori_loop(1, 32, greet, 0)

    loads[14].wait()
    place = 40 * (t // 2)
    base = jnp.minimum(place // 128, 8) * 128
    lane = lax.broadcasted_iota(jnp.int32, (256, 128), 1)
    row = lax.broadcasted_iota(jnp.int32, (256, 128), 0)
    piece, step = lane // 32, lane % 32
    wanted = place - base + step + 20 * jnp.where(piece == 0, c, 1 - c)
    pick = jnp.where((row == wanted) & (lane < 64) & (step < 20), 1.0, 0.0).astype(BF16)
    for to in range(G):
        window = hv[:, pl.ds(pl.multiple_of(1280 * to + base, 128), 256)]
        hsend[to] = jnp.dot(window, pick, preferred_element_type=F32)

    def sums(ref, rows, width, step):
        def body(i, acc):
            at = pl.ds(pl.multiple_of(i * step, step), step)
            init = ref[0, :, at].astype(F32)
            a = ref[1, :, at].astype(F32) - init
            b = ref[2, :, at].astype(F32) - init
            return (acc[0] + a * a, acc[1] + b * b, acc[2] + a * b)

        zero = jnp.zeros((rows, step), F32)
        totals = lax.fori_loop(0, width // step, body, (zero, zero, zero), unroll=2)
        done = []
        for total in totals:
            line = jnp.sum(total, axis=0, keepdims=True)
            done.append(sum(line[:, 128 * j : 128 * (j + 1)] for j in range(step // 128)))
        return done

    sub16 = lax.broadcasted_iota(jnp.int32, (16, 128), 0)
    lane16 = lax.broadcasted_iota(jnp.int32, (16, 128), 1)
    stack = jnp.zeros((16, 128), F32)
    for m, (ref, rows, width) in enumerate(
        ((wq, DEPTH, QW), (wk, DEPTH, KW), (wv, DEPTH, KW), (wo, ODEPTH, OW))
    ):
        for j in range(3):
            loads[3 * m + j].wait()
        for kind, line in enumerate(sums(ref, rows, width, 256)):
            stack = jnp.where(sub16 == 4 * kind + m, line, stack)
    stack = jnp.sum(stack, axis=1, keepdims=True)
    sa[...] = jnp.sum(jnp.where(sub16 == lane16, stack, 0.0), axis=0, keepdims=True)

    pl.semaphore_wait(barrier, 46)

    def to_plane(src, dst, stage):
        def body(i, _):
            there = (xy + i) % XY
            remote(src(there), dst, stage, (g, there * 4 + w)).start()
            return 0

        lax.fori_loop(1, XY, body, 0)

    to_plane(lambda there: sa, ra.at[xy], 1)
    ra[xy] = sa[...]

    other = (g, t + 1 - 2 * c)
    swaps = []
    for m, width in enumerate((QW // 2, KW // 2, KW // 2, OW // 2)):
        for j in range(3):
            start = pl.multiple_of((1 - c) * width, 128)
            swaps.append(
                pltpu.make_async_remote_copy(
                    src_ref=raw[m][j].at[:, pl.ds(start, width)], dst_ref=theirs[m].at[j],
                    send_sem=swap_send.at[3 * m + j], recv_sem=swap_recv.at[3 * m + j],
                    device_id=other, device_id_type=MESH,
                )
            )
    for i in range(1, G):
        to = (g + i) % G
        remote(hsend.at[to], hrecv.at[g], 0, (to, t)).start()
    hrecv[g] = hsend[g]
    for copy in swaps:
        copy.start()

    def send_caches(i, _):
        place = (xy * 2 + c + i) % 32
        there, core = place // 2, place % 2
        row, kv = (there % 8) // 2, 4 * core + 2 * (there % 2) + there // 8
        device = (g, there * 4 + zh * 2 + core)
        remote(ck.at[row, kv], keys.at[2 * xy + c], 5, device).start()
        remote(cv.at[row, kv], values.at[2 * xy + c], 6, device).start()
        return 0

    lax.fori_loop(1, 32, send_caches, 0)

    settle(ra.at[pl.ds(0, XY - 1)], recv_sem.at[1])
    sb[...] = jnp.sum(ra[...], axis=0)

    def send_sums(i, _):
        remote(sb, rb.at[g * 4 + w], 2, column(i)).start()
        return 0

    lax.fori_loop(1, 16, send_sums, 0)
    rb[g * 4 + w] = sb[...]

    mq[...] = jnp.zeros_like(mq)
    mkv[...] = jnp.zeros_like(mkv)
    settle(hrecv.at[pl.ds(0, G - 1)], recv_sem.at[0])
    for i in range(G):
        hfull[4 * i : 4 * i + 4, :] = hrecv[i]
    rows_all = hfull[...].astype(BF16)[:, :64]
    loads[15].wait()
    loads[16].wait()
    turn = lax.broadcasted_iota(jnp.int32, (8, HD), 1)
    freq = jnp.ones((8, HD), F32)
    for j, value in enumerate(FREQ):
        freq = jnp.where(turn % (HD // 2) == j, float(value), freq)
    angle = pos[my_row].astype(F32) * freq
    cosine = jnp.cos(angle)
    sine = jnp.sin(angle)
    sine = jnp.where(turn < HD // 2, -sine, sine)

    def rotate(value):
        return value * cosine + pltpu.roll(value, HD // 2, 1) * sine

    for copy in swaps:
        copy.wait_recv()

    settle(rb.at[pl.ds(0, 15)], recv_sem.at[2])
    total = jnp.broadcast_to(jnp.sum(rb[...], axis=0), (8, 128))
    bb = pltpu.roll(total, 124, 1)
    ab = pltpu.roll(total, 120, 1)
    similar = ab / jnp.sqrt(total * bb + 1e-06)
    share = 1.0 / jnp.sqrt(2.0 * (1.0 + similar))
    lane8 = lax.broadcasted_iota(jnp.int32, (8, 128), 1)
    shares = [
        jnp.sum(jnp.where(lane8 == m, share, 0.0), axis=1, keepdims=True)[0:1] for m in range(4)
    ]

    def merge(init, first, second, factor):
        base = init.astype(F32)
        a = first.astype(F32) - base
        b = second.astype(F32) - base
        return (base + factor * a + factor * b).astype(BF16)

    def merge_into(dst, offset, own, swapped, own_row, other_row, width, factor, step):
        def body(i, _):
            there = pl.ds(pl.multiple_of(i * step, step), step)
            here = pl.ds(pl.multiple_of(c * width + i * step, step), step)
            to = pl.ds(pl.multiple_of(offset + i * step, step), step)
            dst[own_row, to] = merge(own[0, :, here], own[1, :, here], own[2, :, here], factor)
            dst[other_row, to] = merge(
                swapped[0, :, there], swapped[1, :, there], swapped[2, :, there], factor
            )
            return 0

        lax.fori_loop(0, width // step, body, 0, unroll=2)

    top, bottom = pl.ds(0, DEPTH), pl.ds(32, DEPTH)
    merge_into(mq, 0, wq, pq, top, bottom, QW // 2, shares[0], 256)

    flat = qsend.reshape(4 * 16 * 8, HD)
    for kind in range(4):
        for half in range(2):
            start = 1024 * kind + 512 * half
            part = jnp.dot(rows_all, mq[:, start : start + 512], preferred_element_type=F32)
            for j in range(4):
                at = pl.ds(128 * kind + 4 * half + j, 16, stride=8)
                flat[at, :] = part[:, 128 * j : 128 * (j + 1)]

    def piece_for(there):
        return (2 * (there % 2) + there // 8, slice(None), (there % 8) // 2)

    to_plane(lambda there: qsend.at[piece_for(there)], qrecv.at[xy], 3)
    qrecv[xy] = qsend[my_kind, :, my_row]

    merge_into(mkv, 0, wk, pk, top, bottom, KW // 2, shares[1], 256)
    merge_into(mkv, KW // 2, wv, pv, top, bottom, KW // 2, shares[2], 256)
    new = jnp.dot(rows_all, mkv[...], preferred_element_type=F32)
    for kind in range(4):
        for i in range(16):
            for j in range(2):
                start = 512 * j + 128 * kind
                ksend[kind, i // 4, i % 4, j : j + 1] = new[i : i + 1, start : start + 128]
    to_plane(lambda there: ksend.at[piece_for(there)], krecv.at[xy], 11)
    krecv[xy] = ksend[my_kind, :, my_row]

    merge_into(
        mo, 0, wo, po, pl.ds(pl.multiple_of(32 * c, 32), 32),
        pl.ds(pl.multiple_of(32 * (1 - c), 32), 32), OW // 2, shares[3], 256,
    )

    def to_z(src, dst, stage):
        def body(i, _):
            there = (z + i) % 8
            group = there % 4
            remote(src(group), dst, stage, (group, xy * 4 + (there // 4) * 2 + c)).start()
            return 0

        lax.fori_loop(1, 8, body, 0)

    settle(qrecv.at[pl.ds(0, XY - 1)], recv_sem.at[3])
    zsend[...] = jnp.sum(qrecv[...], axis=0)
    to_z(lambda group: zsend.at[group], zrecv.at[z], 4)
    zrecv[z] = zsend[g]
    settle(krecv.at[pl.ds(0, XY - 1)], recv_sem.at[11])
    nsend[...] = jnp.sum(krecv[...], axis=0)
    to_z(lambda group: nsend.at[group], nrecv.at[z], 12)
    nrecv[z] = nsend[g]

    loads[12].wait()
    loads[13].wait()
    settle(keys.at[pl.ds(0, 31)], recv_sem.at[5])
    settle(values.at[pl.ds(0, 31)], recv_sem.at[6])
    settle(zrecv.at[pl.ds(0, 7)], recv_sem.at[4])
    query = rotate(jnp.sum(zrecv[...], axis=0)).astype(BF16)
    length = lens[my_row]
    lane = lax.broadcasted_iota(jnp.int32, (8, 128), 1)
    low = lane < SPAN
    scores, peaks = [], []
    for chunk in range(8):
        score = lax.dot_general(
            query, keys[4 * chunk : 4 * chunk + 4].reshape(4 * SPAN, HD),
            (((1,), (1,)), ((), ())), preferred_element_type=F32,
        )
        for i in range(2):
            slot = (4 * (2 * chunk + i) + 2 * zh) * SPAN + lane
            valid = slot < length
            part = jnp.where(valid, score[:, 128 * i : 128 * (i + 1)] * SCALE, -1e30)
            left = jnp.max(jnp.where(low, part, -1e30), axis=1, keepdims=True)
            right = jnp.max(jnp.where(low, -1e30, part), axis=1, keepdims=True)
            scores.append((part, valid))
            peaks.append(jnp.where(low, left, right))
    most = peaks[0]
    for peak in peaks[1:]:
        most = jnp.maximum(most, peak)
    most = jnp.maximum(most, pltpu.roll(most, 64, 1))
    mass = jnp.zeros((8, 128), F32)
    mixed = jnp.zeros((24, HD), F32)
    for chunk in range(8):
        terms = []
        for i in range(2):
            (part, valid), peak = scores[2 * chunk + i], peaks[2 * chunk + i]
            weight = jnp.where(valid, jnp.exp(part - peak), 0.0).astype(BF16).astype(F32)
            weight = weight * jnp.exp(peak - most)
            mass = mass + weight
            first = weight.astype(BF16)
            rest = weight - first.astype(F32)
            second = rest.astype(BF16)
            third = (rest - second.astype(F32)).astype(BF16)
            terms.append(jnp.concatenate([first, second, third], axis=0))
        mixed = mixed + jnp.dot(
            jnp.concatenate(terms, axis=1),
            values[4 * chunk : 4 * chunk + 4].reshape(4 * SPAN, HD),
            preferred_element_type=F32,
        )
    mixed = mixed[0:8] + mixed[8:16] + mixed[16:24]
    mass = jnp.sum(mass, axis=1, keepdims=True)
    most = most[:, 0:1]

    settle(nrecv.at[pl.ds(0, 7)], recv_sem.at[12])
    new = jnp.sum(nrecv[...], axis=0)
    new_key = jnp.broadcast_to(new[0:1], (8, HD))
    new_key = rotate(new_key).astype(BF16).astype(F32)
    new_value = new[1:2].astype(BF16).astype(F32)
    own = jnp.sum(query.astype(F32) * new_key, axis=1, keepdims=True) * SCALE
    own = jnp.where(zh == 0, own, most)
    peak = jnp.maximum(most, own)
    old = jnp.exp(most - peak)
    fresh = jnp.where(zh == 0, jnp.exp(own - peak), 0.0)
    mixed = mixed * old + fresh * new_value
    stats = jnp.where(low, peak, mass * old + fresh)
    for j in range(8):
        asend[j, 0:1] = mixed[j : j + 1]
        asend[j, 1:2] = stats[j : j + 1]

    owner = my_kv // 2
    slot = (4 * g + my_row) * 2 + zh

    def send_heads(i, _):
        place = (xy % 8 * 4 + w + i) % 32
        j = place // 4
        device = (owner, ((xy // 8) * 8 + j) * 4 + place % 4)
        remote(asend.at[j], arecv.at[slot], 7, device).start()
        return 0

    lax.fori_loop(1, 32, send_heads, 0)

    @pl.when(owner != g)
    def _():
        remote(asend.at[xy % 8], arecv.at[slot], 7, (owner, t)).start()
        settle(arecv, recv_sem.at[7])

    @pl.when(owner == g)
    def _():
        arecv[slot] = asend[xy % 8]
        settle(arecv.at[pl.ds(0, 31)], recv_sem.at[7])

    for i in range(16):
        for side in range(2):
            hd[2 * side, i : i + 1] = arecv[2 * i + side, 0:1]
            hd[2 * side + 1, i : i + 1] = arecv[2 * i + side, 1:2]
    left, right = hd[1], hd[3]
    most = jnp.maximum(left[:, 0:1], right[:, 0:1])
    left_factor = jnp.exp(left[:, 0:1] - most)
    right_factor = jnp.exp(right[:, 0:1] - most)
    heads = (hd[0] * left_factor + hd[2] * right_factor) / (
        left[:, 64:65] * left_factor + right[:, 64:65] * right_factor
    )
    heads = jnp.where(zh == 1, pltpu.roll(heads, 64, 1), heads).astype(BF16)[:, :64]

    for tile in range(20):
        part = jnp.dot(
            heads, mo[:, 128 * tile : 128 * (tile + 1)], preferred_element_type=F32
        )
        for i in range(G):
            if tile < XY:
                bsend[tile, i] = part[4 * i : 4 * i + 4]
            else:
                bsend[4 * i + tile - XY, 4] = part[4 * i : 4 * i + 4]
    to_plane(lambda there: bsend.at[there], brecv.at[xy], 8)
    brecv[xy] = bsend[xy]
    settle(brecv.at[pl.ds(0, XY - 1)], recv_sem.at[8])
    total = jnp.sum(brecv[...], axis=0)
    for i in range(G):
        ysend[i, 0] = total[i]
        ysend[i, 1] = total[4]
    to_z(lambda group: ysend.at[group], yrecv.at[z], 9)
    yrecv[z] = ysend[g]
    settle(yrecv.at[pl.ds(0, 7)], recv_sem.at[9])
    osend[...] = jnp.sum(yrecv[...], axis=0)

    def send_out(i, _):
        remote(osend, obuf.at[c * 16 + xy], 10, plane(i)).start()
        return 0

    lax.fori_loop(1, 32, send_out, 0)
    obuf[c * 16 + xy] = osend[...]
    settle(obuf.at[pl.ds(0, 31)], recv_sem.at[10])
    for core in range(2):
        for tile in range(20):
            start = core * (OW // 2) + 128 * tile
            if tile < XY:
                value = obuf[core * 16 + tile, 0]
            else:
                value = obuf[core * 16 + 4 * g + tile - XY, 1]
            out[:, start : start + 128] = value.astype(out.dtype)

    for copy in swaps:
        copy.wait_send()
    for stage, ref, count in (
        (0, hrecv, 3), (1, ra, 15), (2, rb, 15), (3, qrecv, 15), (4, zrecv, 7), (5, keys, 31),
        (6, values, 31), (8, brecv, 15), (9, yrecv, 7), (10, obuf, 31), (11, krecv, 15), (12, nrecv, 7),
    ):
        settle(ref.at[pl.ds(0, count)], send_sem.at[stage])
    settle(arecv.at[pl.ds(0, 31)], send_sem.at[7])

    @pl.when(owner != g)
    def _():
        settle(arecv.at[0], send_sem.at[7])


def shards(*args):
    hbm, vmem = (pl.BlockSpec(memory_space=space) for space in (pltpu.HBM, pltpu.VMEM))
    f32 = lambda *shape: pltpu.VMEM(shape, F32)
    bf16 = lambda *shape: pltpu.VMEM(shape, BF16)
    return pl.pallas_call(
        kernel,
        out_shape=jax.ShapeDtypeStruct((R, OW), BF16),
        in_specs=[hbm] * 17,
        out_specs=vmem,
        scratch_shapes=[
            pltpu.SMEM((R,), jnp.int32), pltpu.SMEM((R,), jnp.int32),
            bf16(3, DEPTH, QW), bf16(3, DEPTH, KW), bf16(3, DEPTH, KW), bf16(3, ODEPTH, OW),
            bf16(3, DEPTH, QW // 2), bf16(3, DEPTH, KW // 2), bf16(3, DEPTH, KW // 2), bf16(3, ODEPTH, OW // 2),
            bf16(32, SPAN, HD), bf16(32, SPAN, HD), bf16(R, 5120),
            f32(G, R, HD), f32(G, R, HD), f32(16, HD),
            f32(1, HD), f32(XY, 1, HD), f32(1, HD), f32(16, 1, HD),
            bf16(64, QW // 2), bf16(64, KW), bf16(64, OW // 2),
            f32(4, G, R, 8, HD), f32(XY, G, 8, HD), f32(4, G, R, 2, HD), f32(XY, G, 2, HD),
            f32(G, 8, HD), f32(8, 8, HD), f32(G, 2, HD), f32(8, 2, HD),
            f32(8, 2, HD), f32(32, 2, HD), f32(4, 16, HD),
            f32(XY, 5, R, HD), f32(XY, 5, R, HD), f32(G, 2, R, HD), f32(8, 2, R, HD),
            f32(2, R, HD), f32(32, 2, R, HD),
            pltpu.SemaphoreType.DMA((17,)), pltpu.SemaphoreType.DMA((12,)), pltpu.SemaphoreType.DMA((12,)),
            pltpu.SemaphoreType.DMA((13,)), pltpu.SemaphoreType.DMA((13,)),
        ],
        compiler_params=pltpu.CompilerParams(
            collective_id=0, has_side_effects=True, vmem_limit_bytes=56 * 1024 * 1024
        ),
        cost_estimate=pl.CostEstimate(flops=40_000_000, bytes_accessed=4_000_000, transcendentals=100_000),
    )(*args)


def solution(mesh):
    both = P(("group", "tensor"), None)
    cache = P("group", None, "tensor", None)
    in_specs = (both,) * 12 + (P("group", None), cache, cache, P("group"), P("group"))
    return jax.shard_map(
        shards, mesh=mesh, in_specs=in_specs, out_specs=P("group", None), check_vma=False
    )
```

```python
import math

import jax
import jax.numpy as jnp
import numpy as np
from jax import lax
from jax.experimental import pallas as pl
from jax.experimental.pallas import tpu as pltpu
from jax.sharding import PartitionSpec as P

MESH = pl.DeviceIdType.MESH
F32 = jnp.float32
BF16 = jnp.bfloat16
G, XY, W = 4, 16, 4
R, HD, SPAN = 4, 128, 64
QW, KW, OW = 8192, 1024, 5120
DEPTH, ODEPTH = 20, 32
FREQ = (1000000.0 ** (-np.arange(HD // 2) / (HD // 2))).astype(np.float32)


def ring(step, size):
    return min(step, size - step)


PLANE = sorted(((a, b) for a in range(4) for b in range(4)), key=lambda s: -ring(s[0], 4) - ring(s[1], 4))
PLANE_CORES = sorted(
    ((a, b, k) for a, b in PLANE for k in range(2)),
    key=lambda s: -ring(s[0], 4) - ring(s[1], 4) - 0.1 * s[2],
)
LINE = sorted(range(8), key=lambda s: -ring(s, 8))
COLUMN = sorted(((a, k) for a in LINE for k in range(2)), key=lambda s: -ring(s[0], 8) - 0.1 * s[1])
OWNERS = sorted(
    ((a, b, e, k) for a in range(2) for b in range(4) for e in range(2) for k in range(2)),
    key=lambda s: -s[0] - ring(s[1], 4) - 3 * s[2] - 0.1 * s[3],
)
SCALE = 1.0 / math.sqrt(HD)


def kernel(
    qi, qf, qs, ki, kf, ks, vi, vf, vs, oi, of, os_, hid, ck, cv, pos_in, lens_in,
    out,
    pos, lens,
    wq, wk, wv, wo, pq, pk, pv, po, keys, values, hv,
    hsend, hrecv, hfull, sa, ra, sb, rb, mq, mkv, mo,
    qsend, qrecv, ksend, krecv, zsend, zrecv, nsend, nrecv,
    asend, arecv, hd, bsend, brecv, ysend, yrecv, osend, obuf,
    load_sem, swap_send, swap_recv, send_sem, recv_sem,
):
    g = lax.axis_index("group")
    t = lax.axis_index("tensor")
    xy, w = lax.div(t, 4), lax.rem(t, 4)
    zh, c = lax.div(w, 2), lax.rem(w, 2)
    x, y = lax.div(xy, 4), lax.rem(xy, 4)
    z = zh * 4 + g
    my_row = 2 * lax.rem(x, 2) + lax.div(y, 2)
    my_kind = 2 * lax.rem(y, 2) + lax.div(x, 2)
    my_kv = 4 * c + my_kind

    def remote(src, dst, stage, device):
        return pltpu.make_async_remote_copy(
            src_ref=src, dst_ref=dst, send_sem=send_sem.at[stage], recv_sem=recv_sem.at[stage],
            device_id=device, device_id_type=MESH,
        )

    def settle(ref, sem):
        pltpu.make_async_copy(ref, ref, sem).wait()

    raw = [(qi, qf, qs), (ki, kf, ks), (vi, vf, vs), (oi, of, os_)]
    mine = [wq, wk, wv, wo]
    theirs = [pq, pk, pv, po]
    loads = []
    for m in range(4):
        for j in range(3):
            loads.append(pltpu.make_async_copy(raw[m][j], mine[m].at[j], load_sem.at[3 * m + j]))
    place = 2 * xy + c
    loads.append(pltpu.make_async_copy(ck.at[my_row, my_kv], keys.at[place], load_sem.at[12]))
    loads.append(pltpu.make_async_copy(cv.at[my_row, my_kv], values.at[place], load_sem.at[13]))
    loads.append(pltpu.make_async_copy(hid, hv, load_sem.at[14]))
    loads.append(pltpu.make_async_copy(pos_in, pos, load_sem.at[15]))
    loads.append(pltpu.make_async_copy(lens_in, lens, load_sem.at[16]))
    for copy in loads:
        copy.start()

    rem, div = lax.rem, lax.div

    def chip(a, b):
        return rem(x + a, 4) * 4 + rem(y + b, 4)

    def column(a, k):
        there = rem(z + a, 8)
        return (rem(there, 4), xy * 4 + div(there, 4) * 2 + rem(c + k, 2))

    barrier = pltpu.get_barrier_semaphore()
    for a, k in COLUMN[:-1]:
        pl.semaphore_signal(barrier, inc=1, device_id=column(a, k), device_id_type=MESH)
    for a, b in PLANE[:-1]:
        there = (g, chip(a, b) * 4 + w)
        pl.semaphore_signal(barrier, inc=1, device_id=there, device_id_type=MESH)

    loads[14].wait()
    place = 40 * (t // 2)
    base = jnp.minimum(place // 128, 8) * 128
    lane = lax.broadcasted_iota(jnp.int32, (256, 128), 1)
    row = lax.broadcasted_iota(jnp.int32, (256, 128), 0)
    piece, step = lane // 32, lane % 32
    wanted = place - base + step + 20 * jnp.where(piece == 0, c, 1 - c)
    pick = jnp.where((row == wanted) & (lane < 64) & (step < 20), 1.0, 0.0).astype(BF16)
    for to in range(G):
        window = hv[:, pl.ds(pl.multiple_of(1280 * to + base, 128), 256)]
        hsend[to] = jnp.dot(window, pick, preferred_element_type=F32)

    def sums(ref, rows, width, step):
        def body(i, acc):
            at = pl.ds(pl.multiple_of(i * step, step), step)
            init = ref[0, :, at].astype(F32)
            a = ref[1, :, at].astype(F32) - init
            b = ref[2, :, at].astype(F32) - init
            return (acc[0] + a * a, acc[1] + b * b, acc[2] + a * b)

        zero = jnp.zeros((rows, step), F32)
        totals = lax.fori_loop(0, width // step, body, (zero, zero, zero), unroll=2)
        done = []
        for total in totals:
            line = jnp.sum(total, axis=0, keepdims=True)
            done.append(sum(line[:, 128 * j : 128 * (j + 1)] for j in range(step // 128)))
        return done

    sub16 = lax.broadcasted_iota(jnp.int32, (16, 128), 0)
    lane16 = lax.broadcasted_iota(jnp.int32, (16, 128), 1)
    stack = jnp.zeros((16, 128), F32)
    for m, (ref, rows, width) in enumerate(
        ((wq, DEPTH, QW), (wk, DEPTH, KW), (wv, DEPTH, KW), (wo, ODEPTH, OW))
    ):
        for j in range(3):
            loads[3 * m + j].wait()
        for kind, line in enumerate(sums(ref, rows, width, 256)):
            stack = jnp.where(sub16 == 4 * kind + m, line, stack)
    stack = jnp.sum(stack, axis=1, keepdims=True)
    sa[...] = jnp.sum(jnp.where(sub16 == lane16, stack, 0.0), axis=0, keepdims=True)

    pl.semaphore_wait(barrier, 30)

    def to_plane(src, dst, stage):
        for a, b in PLANE[:-1]:
            there = chip(a, b)
            remote(src(there), dst, stage, (g, there * 4 + w)).start()

    to_plane(lambda there: sa, ra.at[xy], 1)
    ra[xy] = sa[...]

    other = (g, t + 1 - 2 * c)
    swaps = []
    for m, width in enumerate((QW // 2, KW // 2, KW // 2, OW // 2)):
        for j in range(3):
            start = pl.multiple_of((1 - c) * width, 128)
            swaps.append(
                pltpu.make_async_remote_copy(
                    src_ref=raw[m][j].at[:, pl.ds(start, width)], dst_ref=theirs[m].at[j],
                    send_sem=swap_send.at[3 * m + j], recv_sem=swap_recv.at[3 * m + j],
                    device_id=other, device_id_type=MESH,
                )
            )
    for i in range(1, G):
        to = rem(g + i, G)
        remote(hsend.at[to], hrecv.at[g], 0, (to, t)).start()
    hrecv[g] = hsend[g]
    for copy in swaps:
        copy.start()

    def send_cache(src, dst, stage, core, first, last):
        for a, b in PLANE[first:last]:
            to_x, to_y = rem(x + a, 4), rem(y + b, 4)
            row = 2 * rem(to_x, 2) + div(to_y, 2)
            kv = 4 * core + 2 * rem(to_y, 2) + div(to_x, 2)
            device = (g, (4 * to_x + to_y) * 4 + zh * 2 + core)
            remote(src.at[row, kv], dst.at[2 * xy + c], stage, device).start()

    send_cache(ck, keys, 5, c, 0, 15)
    send_cache(cv, values, 6, c, 0, 15)
    settle(ra.at[pl.ds(0, XY - 1)], recv_sem.at[1])
    sb[...] = jnp.sum(ra[...], axis=0)

    for a, k in COLUMN[:-1]:
        remote(sb, rb.at[g * 4 + w], 2, column(a, k)).start()
    rb[g * 4 + w] = sb[...]

    send_cache(ck, keys, 5, 1 - c, 0, 16)
    send_cache(cv, values, 6, 1 - c, 0, 8)
    mq[...] = jnp.zeros_like(mq)
    mkv[...] = jnp.zeros_like(mkv)
    settle(hrecv.at[pl.ds(0, G - 1)], recv_sem.at[0])
    for i in range(G):
        hfull[4 * i : 4 * i + 4, :] = hrecv[i]
    rows_all = hfull[...].astype(BF16)[:, :64]
    loads[15].wait()
    loads[16].wait()
    turn = lax.broadcasted_iota(jnp.int32, (8, HD), 1)
    freq = jnp.ones((8, HD), F32)
    for j, value in enumerate(FREQ):
        freq = jnp.where(turn % (HD // 2) == j, float(value), freq)
    angle = pos[my_row].astype(F32) * freq
    cosine = jnp.cos(angle)
    sine = jnp.sin(angle)
    sine = jnp.where(turn < HD // 2, -sine, sine)

    def rotate(value):
        return value * cosine + pltpu.roll(value, HD // 2, 1) * sine

    for copy in swaps:
        copy.wait_recv()

    settle(rb.at[pl.ds(0, 15)], recv_sem.at[2])
    total = jnp.broadcast_to(jnp.sum(rb[...], axis=0), (8, 128))
    bb = pltpu.roll(total, 124, 1)
    ab = pltpu.roll(total, 120, 1)
    similar = ab / jnp.sqrt(total * bb + 1e-06)
    share = 1.0 / jnp.sqrt(2.0 * (1.0 + similar))
    lane8 = lax.broadcasted_iota(jnp.int32, (8, 128), 1)
    shares = [
        jnp.sum(jnp.where(lane8 == m, share, 0.0), axis=1, keepdims=True)[0:1] for m in range(4)
    ]

    def merge(init, first, second, factor):
        base = init.astype(F32)
        a = first.astype(F32) - base
        b = second.astype(F32) - base
        return (base + factor * a + factor * b).astype(BF16)

    def merge_into(dst, offset, own, swapped, own_row, other_row, width, factor, step):
        def body(i, _):
            there = pl.ds(pl.multiple_of(i * step, step), step)
            here = pl.ds(pl.multiple_of(c * width + i * step, step), step)
            to = pl.ds(pl.multiple_of(offset + i * step, step), step)
            dst[own_row, to] = merge(own[0, :, here], own[1, :, here], own[2, :, here], factor)
            dst[other_row, to] = merge(
                swapped[0, :, there], swapped[1, :, there], swapped[2, :, there], factor
            )
            return 0

        lax.fori_loop(0, width // step, body, 0, unroll=2)

    top, bottom = pl.ds(0, DEPTH), pl.ds(32, DEPTH)
    merge_into(mq, 0, wq, pq, top, bottom, QW // 2, shares[0], 256)

    flat = qsend.reshape(4 * 16 * 8, HD)
    for kind in range(4):
        for half in range(2):
            start = 1024 * kind + 512 * half
            part = jnp.dot(rows_all, mq[:, start : start + 512], preferred_element_type=F32)
            for j in range(4):
                at = pl.ds(128 * kind + 4 * half + j, 16, stride=8)
                flat[at, :] = part[:, 128 * j : 128 * (j + 1)]

    def piece_for(there):
        return (2 * rem(there, 2) + div(there, 8), slice(None), div(rem(there, 8), 2))

    to_plane(lambda there: qsend.at[piece_for(there)], qrecv.at[xy], 3)
    qrecv[xy] = qsend[my_kind, :, my_row]

    merge_into(mkv, 0, wk, pk, top, bottom, KW // 2, shares[1], 256)
    merge_into(mkv, KW // 2, wv, pv, top, bottom, KW // 2, shares[2], 256)
    new = jnp.dot(rows_all, mkv[...], preferred_element_type=F32)
    flat_new = ksend.reshape(4 * 16 * 2, HD)
    for kind in range(4):
        for j in range(2):
            start = 512 * j + 128 * kind
            flat_new[pl.ds(32 * kind + j, 16, stride=2), :] = new[:, start : start + 128]
    to_plane(lambda there: ksend.at[piece_for(there)], krecv.at[xy], 11)
    krecv[xy] = ksend[my_kind, :, my_row]

    merge_into(
        mo, 0, wo, po, pl.ds(pl.multiple_of(32 * c, 32), 32),
        pl.ds(pl.multiple_of(32 * (1 - c), 32), 32), OW // 2, shares[3], 256,
    )

    def to_z(src, dst, stage):
        for a in LINE[:-1]:
            device = column(a, 0)
            remote(src(device[0]), dst, stage, device).start()

    settle(qrecv.at[pl.ds(0, XY - 1)], recv_sem.at[3])
    zsend[...] = jnp.sum(qrecv[...], axis=0)
    to_z(lambda group: zsend.at[group], zrecv.at[z], 4)
    zrecv[z] = zsend[g]
    send_cache(cv, values, 6, 1 - c, 8, 16)
    settle(krecv.at[pl.ds(0, XY - 1)], recv_sem.at[11])
    nsend[...] = jnp.sum(krecv[...], axis=0)
    to_z(lambda group: nsend.at[group], nrecv.at[z], 12)
    nrecv[z] = nsend[g]

    loads[12].wait()
    loads[13].wait()
    settle(keys.at[pl.ds(0, 31)], recv_sem.at[5])
    settle(values.at[pl.ds(0, 31)], recv_sem.at[6])
    settle(zrecv.at[pl.ds(0, 7)], recv_sem.at[4])
    query = rotate(jnp.sum(zrecv[...], axis=0)).astype(BF16)
    length = lens[my_row]
    lane = lax.broadcasted_iota(jnp.int32, (8, 128), 1)
    low = lane < SPAN
    scores, peaks = [], []
    for chunk in range(8):
        score = lax.dot_general(
            query, keys[4 * chunk : 4 * chunk + 4].reshape(4 * SPAN, HD),
            (((1,), (1,)), ((), ())), preferred_element_type=F32,
        )
        for i in range(2):
            slot = (4 * (2 * chunk + i) + 2 * zh) * SPAN + lane
            valid = slot < length
            part = jnp.where(valid, score[:, 128 * i : 128 * (i + 1)] * SCALE, -1e30)
            left = jnp.max(jnp.where(low, part, -1e30), axis=1, keepdims=True)
            right = jnp.max(jnp.where(low, -1e30, part), axis=1, keepdims=True)
            scores.append((part, valid))
            peaks.append(jnp.where(low, left, right))
    most = peaks[0]
    for peak in peaks[1:]:
        most = jnp.maximum(most, peak)
    most = jnp.maximum(most, pltpu.roll(most, 64, 1))
    mass = jnp.zeros((8, 128), F32)
    mixed = jnp.zeros((24, HD), F32)
    for chunk in range(8):
        terms = []
        for i in range(2):
            (part, valid), peak = scores[2 * chunk + i], peaks[2 * chunk + i]
            weight = jnp.where(valid, jnp.exp(part - peak), 0.0).astype(BF16).astype(F32)
            weight = weight * jnp.exp(peak - most)
            mass = mass + weight
            first = weight.astype(BF16)
            rest = weight - first.astype(F32)
            second = rest.astype(BF16)
            third = (rest - second.astype(F32)).astype(BF16)
            terms.append(jnp.concatenate([first, second, third], axis=0))
        mixed = mixed + jnp.dot(
            jnp.concatenate(terms, axis=1),
            values[4 * chunk : 4 * chunk + 4].reshape(4 * SPAN, HD),
            preferred_element_type=F32,
        )
    mixed = mixed[0:8] + mixed[8:16] + mixed[16:24]
    mass = jnp.sum(mass, axis=1, keepdims=True)
    most = most[:, 0:1]

    settle(nrecv.at[pl.ds(0, 7)], recv_sem.at[12])
    new = jnp.sum(nrecv[...], axis=0)
    new_key = jnp.broadcast_to(new[0:1], (8, HD))
    new_key = rotate(new_key).astype(BF16).astype(F32)
    new_value = new[1:2].astype(BF16).astype(F32)
    own = jnp.sum(query.astype(F32) * new_key, axis=1, keepdims=True) * SCALE
    own = jnp.where(zh == 0, own, most)
    peak = jnp.maximum(most, own)
    old = jnp.exp(most - peak)
    fresh = jnp.where(zh == 0, jnp.exp(own - peak), 0.0)
    mixed = mixed * old + fresh * new_value
    stats = jnp.where(low, peak, mass * old + fresh)
    for j in range(8):
        asend[j, 0:1] = mixed[j : j + 1]
        asend[j, 1:2] = stats[j : j + 1]

    owner = lax.div(my_kv, 2)
    slot = (4 * g + my_row) * 2 + zh

    for a, b, e, k in OWNERS[:-1]:
        j = 4 * rem(x + a, 2) + rem(y + b, 4)
        device = (owner, (div(x, 2) * 8 + j) * 4 + 2 * rem(zh + e, 2) + rem(c + k, 2))
        remote(asend.at[j], arecv.at[slot], 7, device).start()

    @pl.when(owner != g)
    def _():
        remote(asend.at[rem(xy, 8)], arecv.at[slot], 7, (owner, t)).start()
        settle(arecv, recv_sem.at[7])

    @pl.when(owner == g)
    def _():
        arecv[slot] = asend[rem(xy, 8)]
        settle(arecv.at[pl.ds(0, 31)], recv_sem.at[7])

    for i in range(16):
        for side in range(2):
            hd[2 * side, i : i + 1] = arecv[2 * i + side, 0:1]
            hd[2 * side + 1, i : i + 1] = arecv[2 * i + side, 1:2]
    left, right = hd[1], hd[3]
    most = jnp.maximum(left[:, 0:1], right[:, 0:1])
    left_factor = jnp.exp(left[:, 0:1] - most)
    right_factor = jnp.exp(right[:, 0:1] - most)
    heads = (hd[0] * left_factor + hd[2] * right_factor) / (
        left[:, 64:65] * left_factor + right[:, 64:65] * right_factor
    )
    heads = jnp.where(zh == 1, pltpu.roll(heads, 64, 1), heads).astype(BF16)[:, :64]

    for tile in range(20):
        part = jnp.dot(
            heads, mo[:, 128 * tile : 128 * (tile + 1)], preferred_element_type=F32
        )
        for i in range(G):
            if tile < XY:
                bsend[tile, i] = part[4 * i : 4 * i + 4]
            else:
                bsend[4 * i + tile - XY, 4] = part[4 * i : 4 * i + 4]
    to_plane(lambda there: bsend.at[there], brecv.at[xy], 8)
    brecv[xy] = bsend[xy]
    settle(brecv.at[pl.ds(0, XY - 1)], recv_sem.at[8])
    total = jnp.sum(brecv[...], axis=0)
    for i in range(G):
        ysend[i, 0] = total[i]
        ysend[i, 1] = total[4]
    to_z(lambda group: ysend.at[group], yrecv.at[z], 9)
    yrecv[z] = ysend[g]
    settle(yrecv.at[pl.ds(0, 7)], recv_sem.at[9])
    osend[...] = jnp.sum(yrecv[...], axis=0)

    for a, b, k in PLANE_CORES[:-1]:
        device = (g, chip(a, b) * 4 + zh * 2 + rem(c + k, 2))
        remote(osend, obuf.at[c * 16 + xy], 10, device).start()
    obuf[c * 16 + xy] = osend[...]
    settle(obuf.at[pl.ds(0, 31)], recv_sem.at[10])
    for core in range(2):
        for tile in range(20):
            start = core * (OW // 2) + 128 * tile
            if tile < XY:
                value = obuf[core * 16 + tile, 0]
            else:
                value = obuf[core * 16 + 4 * g + tile - XY, 1]
            out[:, start : start + 128] = value.astype(out.dtype)

    for copy in swaps:
        copy.wait_send()
    for stage, ref, count in (
        (0, hrecv, 3), (1, ra, 15), (2, rb, 15), (3, qrecv, 15), (4, zrecv, 7), (5, keys, 31),
        (6, values, 31), (8, brecv, 15), (9, yrecv, 7), (10, obuf, 31), (11, krecv, 15), (12, nrecv, 7),
    ):
        settle(ref.at[pl.ds(0, count)], send_sem.at[stage])
    settle(arecv.at[pl.ds(0, 31)], send_sem.at[7])


    @pl.when(owner != g)
    def _():
        settle(arecv.at[0], send_sem.at[7])


def shards(*args):
    hbm, vmem = (pl.BlockSpec(memory_space=space) for space in (pltpu.HBM, pltpu.VMEM))
    f32 = lambda *shape: pltpu.VMEM(shape, F32)
    bf16 = lambda *shape: pltpu.VMEM(shape, BF16)
    return pl.pallas_call(
        kernel,
        out_shape=jax.ShapeDtypeStruct((R, OW), BF16),
        in_specs=[hbm] * 17,
        out_specs=vmem,
        scratch_shapes=[
            pltpu.SMEM((R,), jnp.int32), pltpu.SMEM((R,), jnp.int32),
            bf16(3, DEPTH, QW), bf16(3, DEPTH, KW), bf16(3, DEPTH, KW), bf16(3, ODEPTH, OW),
            bf16(3, DEPTH, QW // 2), bf16(3, DEPTH, KW // 2), bf16(3, DEPTH, KW // 2), bf16(3, ODEPTH, OW // 2),
            bf16(32, SPAN, HD), bf16(32, SPAN, HD), bf16(R, 5120),
            f32(G, R, HD), f32(G, R, HD), f32(16, HD),
            f32(1, HD), f32(XY, 1, HD), f32(1, HD), f32(16, 1, HD),
            bf16(64, QW // 2), bf16(64, KW), bf16(64, OW // 2),
            f32(4, G, R, 8, HD), f32(XY, G, 8, HD), f32(4, G, R, 2, HD), f32(XY, G, 2, HD),
            f32(G, 8, HD), f32(8, 8, HD), f32(G, 2, HD), f32(8, 2, HD),
            f32(8, 2, HD), f32(32, 2, HD), f32(4, 16, HD),
            f32(XY, 5, R, HD), f32(XY, 5, R, HD), f32(G, 2, R, HD), f32(8, 2, R, HD),
            f32(2, R, HD), f32(32, 2, R, HD),
            pltpu.SemaphoreType.DMA((17,)), pltpu.SemaphoreType.DMA((12,)), pltpu.SemaphoreType.DMA((12,)),
            pltpu.SemaphoreType.DMA((13,)), pltpu.SemaphoreType.DMA((13,)),
        ],
        compiler_params=pltpu.CompilerParams(
            collective_id=0, has_side_effects=True, vmem_limit_bytes=56 * 1024 * 1024
        ),
        cost_estimate=pl.CostEstimate(flops=40_000_000, bytes_accessed=4_000_000, transcendentals=100_000),
    )(*args)


def solution(mesh):
    both = P(("group", "tensor"), None)
    cache = P("group", None, "tensor", None)
    in_specs = (both,) * 12 + (P("group", None), cache, cache, P("group"), P("group"))
    return jax.shard_map(
        shards, mesh=mesh, in_specs=in_specs, out_specs=P("group", None), check_vma=False
    )
```

```python
import math

import jax
import jax.numpy as jnp
import numpy as np
from jax import lax
from jax.experimental import pallas as pl
from jax.experimental.pallas import tpu as pltpu
from jax.sharding import PartitionSpec as P

MESH = pl.DeviceIdType.MESH
F32 = jnp.float32
BF16 = jnp.bfloat16
G, XY, W = 4, 16, 4
R, HD, SPAN = 4, 128, 64
QW, KW, OW = 8192, 1024, 5120
DEPTH, ODEPTH = 20, 32
FREQ = (1000000.0 ** (-np.arange(HD // 2) / (HD // 2))).astype(np.float32)


def ring(step, size):
    return min(step, size - step)


PLANE = sorted(((a, b) for a in range(4) for b in range(4)), key=lambda s: -ring(s[0], 4) - ring(s[1], 4))
NEAR = PLANE[-2::-1] + PLANE[-1:]
PLANE_CORES = sorted(
    ((a, b, k) for a, b in PLANE for k in range(2)),
    key=lambda s: -ring(s[0], 4) - ring(s[1], 4) - 0.1 * s[2],
)
LINE = sorted(range(8), key=lambda s: -ring(s, 8))
COLUMN = sorted(((a, k) for a in LINE for k in range(2)), key=lambda s: -ring(s[0], 8) - 0.1 * s[1])
OWNERS = sorted(
    ((a, b, e, k) for a in range(2) for b in range(4) for e in range(2) for k in range(2)),
    key=lambda s: -s[0] - ring(s[1], 4) - 3 * s[2] - 0.1 * s[3],
)
SCALE = 1.0 / math.sqrt(HD)


def kernel(
    qi, qf, qs, ki, kf, ks, vi, vf, vs, oi, of, os_, hid, ck, cv, pos_in, lens_in,
    out,
    pos, lens,
    wq, wk, wv, wo, pq, pk, pv, po, keys, values, hv,
    hsend, hrecv, hfull, sa, ra, sb, rb, mq, mkv, mo,
    qsend, qrecv, ksend, krecv, zsend, zrecv, nsend, nrecv,
    asend, arecv, hd, bsend, brecv, ysend, yrecv, osend,
    load_sem, swap_send, swap_recv, send_sem, recv_sem,
):
    g = lax.axis_index("group")
    t = lax.axis_index("tensor")
    xy, w = lax.div(t, 4), lax.rem(t, 4)
    zh, c = lax.div(w, 2), lax.rem(w, 2)
    x, y = lax.div(xy, 4), lax.rem(xy, 4)
    z = zh * 4 + g
    my_row = 2 * lax.rem(x, 2) + lax.div(y, 2)
    my_kind = 2 * lax.rem(y, 2) + lax.div(x, 2)
    my_kv = 4 * c + my_kind

    def remote(src, dst, stage, device):
        return pltpu.make_async_remote_copy(
            src_ref=src, dst_ref=dst, send_sem=send_sem.at[stage], recv_sem=recv_sem.at[stage],
            device_id=device, device_id_type=MESH,
        )

    def settle(ref, sem):
        pltpu.make_async_copy(ref, ref, sem).wait()

    raw = [(qi, qf, qs), (ki, kf, ks), (vi, vf, vs), (oi, of, os_)]
    mine = [wq, wk, wv, wo]
    theirs = [pq, pk, pv, po]
    loads = []
    for m in range(4):
        for j in range(3):
            loads.append(pltpu.make_async_copy(raw[m][j], mine[m].at[j], load_sem.at[3 * m + j]))
    place = 2 * xy + c
    loads.append(pltpu.make_async_copy(ck.at[my_row, my_kv], keys.at[place], load_sem.at[12]))
    loads.append(pltpu.make_async_copy(cv.at[my_row, my_kv], values.at[place], load_sem.at[13]))
    loads.append(pltpu.make_async_copy(hid, hv, load_sem.at[14]))
    loads.append(pltpu.make_async_copy(pos_in, pos, load_sem.at[15]))
    loads.append(pltpu.make_async_copy(lens_in, lens, load_sem.at[16]))
    for copy in loads:
        copy.start()

    rem, div = lax.rem, lax.div

    def chip(a, b):
        return rem(x + a, 4) * 4 + rem(y + b, 4)

    def column(a, k):
        there = rem(z + a, 8)
        return (rem(there, 4), xy * 4 + div(there, 4) * 2 + rem(c + k, 2))

    barrier = pltpu.get_barrier_semaphore()
    for a, k in COLUMN[:-1]:
        pl.semaphore_signal(barrier, inc=1, device_id=column(a, k), device_id_type=MESH)
    for a, b in PLANE[:-1]:
        there = (g, chip(a, b) * 4 + w)
        pl.semaphore_signal(barrier, inc=1, device_id=there, device_id_type=MESH)

    loads[14].wait()
    place = 40 * (t // 2)
    base = jnp.minimum(place // 128, 8) * 128
    lane = lax.broadcasted_iota(jnp.int32, (256, 128), 1)
    row = lax.broadcasted_iota(jnp.int32, (256, 128), 0)
    piece, step = lane // 32, lane % 32
    wanted = place - base + step + 20 * jnp.where(piece == 0, c, 1 - c)
    pick = jnp.where((row == wanted) & (lane < 64) & (step < 20), 1.0, 0.0).astype(BF16)
    for to in range(G):
        window = hv[:, pl.ds(pl.multiple_of(1280 * to + base, 128), 256)]
        hsend[to] = jnp.dot(window, pick, preferred_element_type=F32)

    def sums(ref, rows, width, step):
        def body(i, acc):
            at = pl.ds(pl.multiple_of(i * step, step), step)
            init = ref[0, :, at].astype(F32)
            a = ref[1, :, at].astype(F32) - init
            b = ref[2, :, at].astype(F32) - init
            return (acc[0] + a * a, acc[1] + b * b, acc[2] + a * b)

        zero = jnp.zeros((rows, step), F32)
        totals = lax.fori_loop(0, width // step, body, (zero, zero, zero), unroll=2)
        done = []
        for total in totals:
            line = jnp.sum(total, axis=0, keepdims=True)
            done.append(sum(line[:, 128 * j : 128 * (j + 1)] for j in range(step // 128)))
        return done

    sub16 = lax.broadcasted_iota(jnp.int32, (16, 128), 0)
    lane16 = lax.broadcasted_iota(jnp.int32, (16, 128), 1)
    stack = jnp.zeros((16, 128), F32)
    for m, (ref, rows, width) in enumerate(
        ((wq, DEPTH, QW), (wk, DEPTH, KW), (wv, DEPTH, KW), (wo, ODEPTH, OW))
    ):
        for j in range(3):
            loads[3 * m + j].wait()
        for kind, line in enumerate(sums(ref, rows, width, 256)):
            stack = jnp.where(sub16 == 4 * kind + m, line, stack)
    stack = jnp.sum(stack, axis=1, keepdims=True)
    sa[...] = jnp.sum(jnp.where(sub16 == lane16, stack, 0.0), axis=0, keepdims=True)

    pl.semaphore_wait(barrier, 30)

    def to_plane(src, dst, stage):
        for a, b in PLANE[:-1]:
            there = chip(a, b)
            remote(src(there), dst, stage, (g, there * 4 + w)).start()

    to_plane(lambda there: sa, ra.at[xy], 1)
    ra[xy] = sa[...]

    other = (g, t + 1 - 2 * c)
    swaps = []
    for m, width in enumerate((QW // 2, KW // 2, KW // 2, OW // 2)):
        for j in range(3):
            start = pl.multiple_of((1 - c) * width, 128)
            swaps.append(
                pltpu.make_async_remote_copy(
                    src_ref=raw[m][j].at[:, pl.ds(start, width)], dst_ref=theirs[m].at[j],
                    send_sem=swap_send.at[3 * m + j], recv_sem=swap_recv.at[3 * m + j],
                    device_id=other, device_id_type=MESH,
                )
            )
    for i in range(1, G):
        to = rem(g + i, G)
        remote(hsend.at[to], hrecv.at[g], 0, (to, t)).start()
    hrecv[g] = hsend[g]
    for copy in swaps:
        copy.start()

    def send_cache(src, dst, stage, core, first, last):
        for a, b in NEAR[first:last]:
            to_x, to_y = rem(x + a, 4), rem(y + b, 4)
            row = 2 * rem(to_x, 2) + div(to_y, 2)
            kv = 4 * core + 2 * rem(to_y, 2) + div(to_x, 2)
            device = (g, (4 * to_x + to_y) * 4 + zh * 2 + core)
            remote(src.at[row, kv], dst.at[2 * xy + c], stage, device).start()

    send_cache(ck, keys, 5, c, 0, 15)
    send_cache(cv, values, 6, c, 0, 15)
    settle(ra.at[pl.ds(0, XY - 1)], recv_sem.at[1])
    sb[...] = jnp.sum(ra[...], axis=0)

    for a, k in COLUMN[:-1]:
        remote(sb, rb.at[g * 4 + w], 2, column(a, k)).start()
    rb[g * 4 + w] = sb[...]

    send_cache(ck, keys, 5, 1 - c, 0, 16)
    send_cache(cv, values, 6, 1 - c, 0, 8)
    mq[...] = jnp.zeros_like(mq)
    mkv[...] = jnp.zeros_like(mkv)
    settle(hrecv.at[pl.ds(0, G - 1)], recv_sem.at[0])
    for i in range(G):
        hfull[4 * i : 4 * i + 4, :] = hrecv[i]
    rows_all = hfull[...].astype(BF16)[:, :64]
    loads[15].wait()
    loads[16].wait()
    turn = lax.broadcasted_iota(jnp.int32, (8, HD), 1)
    freq = jnp.ones((8, HD), F32)
    for j, value in enumerate(FREQ):
        freq = jnp.where(turn % (HD // 2) == j, float(value), freq)
    angle = pos[my_row].astype(F32) * freq
    cosine = jnp.cos(angle)
    sine = jnp.sin(angle)
    sine = jnp.where(turn < HD // 2, -sine, sine)

    def rotate(value):
        return value * cosine + pltpu.roll(value, HD // 2, 1) * sine

    for copy in swaps:
        copy.wait_recv()

    settle(rb.at[pl.ds(0, 15)], recv_sem.at[2])
    total = jnp.broadcast_to(jnp.sum(rb[...], axis=0), (8, 128))
    bb = pltpu.roll(total, 124, 1)
    ab = pltpu.roll(total, 120, 1)
    similar = ab / jnp.sqrt(total * bb + 1e-06)
    share = 1.0 / jnp.sqrt(2.0 * (1.0 + similar))
    lane8 = lax.broadcasted_iota(jnp.int32, (8, 128), 1)
    shares = [
        jnp.sum(jnp.where(lane8 == m, share, 0.0), axis=1, keepdims=True)[0:1] for m in range(4)
    ]

    def merge(init, first, second, factor):
        base = init.astype(F32)
        a = first.astype(F32) - base
        b = second.astype(F32) - base
        return (base + factor * a + factor * b).astype(BF16)

    def merge_into(dst, offset, own, swapped, own_row, other_row, width, factor, step):
        def body(i, _):
            there = pl.ds(pl.multiple_of(i * step, step), step)
            here = pl.ds(pl.multiple_of(c * width + i * step, step), step)
            to = pl.ds(pl.multiple_of(offset + i * step, step), step)
            dst[own_row, to] = merge(own[0, :, here], own[1, :, here], own[2, :, here], factor)
            dst[other_row, to] = merge(
                swapped[0, :, there], swapped[1, :, there], swapped[2, :, there], factor
            )
            return 0

        lax.fori_loop(0, width // step, body, 0, unroll=2)

    top, bottom = pl.ds(0, DEPTH), pl.ds(32, DEPTH)
    merge_into(mq, 0, wq, pq, top, bottom, QW // 2, shares[0], 256)

    flat = qsend.reshape(4 * 16 * 8, HD)
    for kind in range(4):
        for half in range(2):
            start = 1024 * kind + 512 * half
            part = jnp.dot(rows_all, mq[:, start : start + 512], preferred_element_type=F32)
            for j in range(4):
                at = pl.ds(128 * kind + 4 * half + j, 16, stride=8)
                flat[at, :] = part[:, 128 * j : 128 * (j + 1)]

    def piece_for(there):
        return (2 * rem(there, 2) + div(there, 8), slice(None), div(rem(there, 8), 2))

    to_plane(lambda there: qsend.at[piece_for(there)], qrecv.at[xy], 3)
    qrecv[xy] = qsend[my_kind, :, my_row]

    merge_into(mkv, 0, wk, pk, top, bottom, KW // 2, shares[1], 256)
    merge_into(mkv, KW // 2, wv, pv, top, bottom, KW // 2, shares[2], 256)
    new = jnp.dot(rows_all, mkv[...], preferred_element_type=F32)
    flat_new = ksend.reshape(4 * 16 * 2, HD)
    for kind in range(4):
        for j in range(2):
            start = 512 * j + 128 * kind
            flat_new[pl.ds(32 * kind + j, 16, stride=2), :] = new[:, start : start + 128]
    to_plane(lambda there: ksend.at[piece_for(there)], krecv.at[xy], 11)
    krecv[xy] = ksend[my_kind, :, my_row]

    merge_into(
        mo, 0, wo, po, pl.ds(pl.multiple_of(32 * c, 32), 32),
        pl.ds(pl.multiple_of(32 * (1 - c), 32), 32), OW // 2, shares[3], 256,
    )

    def to_z(src, dst, stage):
        for a in LINE[:-1]:
            device = column(a, 0)
            remote(src(device[0]), dst, stage, device).start()

    settle(qrecv.at[pl.ds(0, XY - 1)], recv_sem.at[3])
    zsend[...] = jnp.sum(qrecv[...], axis=0)
    to_z(lambda group: zsend.at[group], zrecv.at[z], 4)
    zrecv[z] = zsend[g]
    send_cache(cv, values, 6, 1 - c, 8, 16)
    settle(krecv.at[pl.ds(0, XY - 1)], recv_sem.at[11])
    nsend[...] = jnp.sum(krecv[...], axis=0)
    to_z(lambda group: nsend.at[group], nrecv.at[z], 12)
    nrecv[z] = nsend[g]

    loads[12].wait()
    loads[13].wait()
    settle(keys.at[pl.ds(0, 31)], recv_sem.at[5])
    settle(values.at[pl.ds(0, 31)], recv_sem.at[6])
    settle(zrecv.at[pl.ds(0, 7)], recv_sem.at[4])
    query = rotate(jnp.sum(zrecv[...], axis=0)).astype(BF16)
    length = lens[my_row]
    lane = lax.broadcasted_iota(jnp.int32, (8, 128), 1)
    low = lane < SPAN
    scores, peaks = [], []
    for chunk in range(8):
        score = lax.dot_general(
            query, keys[4 * chunk : 4 * chunk + 4].reshape(4 * SPAN, HD),
            (((1,), (1,)), ((), ())), preferred_element_type=F32,
        )
        for i in range(2):
            slot = (4 * (2 * chunk + i) + 2 * zh) * SPAN + lane
            valid = slot < length
            part = jnp.where(valid, score[:, 128 * i : 128 * (i + 1)] * SCALE, -1e30)
            left = jnp.max(jnp.where(low, part, -1e30), axis=1, keepdims=True)
            right = jnp.max(jnp.where(low, -1e30, part), axis=1, keepdims=True)
            scores.append((part, valid))
            peaks.append(jnp.where(low, left, right))
    most = peaks[0]
    for peak in peaks[1:]:
        most = jnp.maximum(most, peak)
    most = jnp.maximum(most, pltpu.roll(most, 64, 1))
    mass = jnp.zeros((8, 128), F32)
    mixed = jnp.zeros((24, HD), F32)
    for chunk in range(8):
        terms = []
        for i in range(2):
            (part, valid), peak = scores[2 * chunk + i], peaks[2 * chunk + i]
            weight = jnp.where(valid, jnp.exp(part - peak), 0.0).astype(BF16).astype(F32)
            weight = weight * jnp.exp(peak - most)
            mass = mass + weight
            first = weight.astype(BF16)
            rest = weight - first.astype(F32)
            second = rest.astype(BF16)
            third = (rest - second.astype(F32)).astype(BF16)
            terms.append(jnp.concatenate([first, second, third], axis=0))
        mixed = mixed + jnp.dot(
            jnp.concatenate(terms, axis=1),
            values[4 * chunk : 4 * chunk + 4].reshape(4 * SPAN, HD),
            preferred_element_type=F32,
        )
    mixed = mixed[0:8] + mixed[8:16] + mixed[16:24]
    mass = jnp.sum(mass, axis=1, keepdims=True)
    most = most[:, 0:1]

    settle(nrecv.at[pl.ds(0, 7)], recv_sem.at[12])
    new = jnp.sum(nrecv[...], axis=0)
    new_key = jnp.broadcast_to(new[0:1], (8, HD))
    new_key = rotate(new_key).astype(BF16).astype(F32)
    new_value = new[1:2].astype(BF16).astype(F32)
    own = jnp.sum(query.astype(F32) * new_key, axis=1, keepdims=True) * SCALE
    own = jnp.where(zh == 0, own, most)
    peak = jnp.maximum(most, own)
    old = jnp.exp(most - peak)
    fresh = jnp.where(zh == 0, jnp.exp(own - peak), 0.0)
    mixed = mixed * old + fresh * new_value
    stats = jnp.where(low, peak, mass * old + fresh)
    for j in range(8):
        asend[j, 0:1] = mixed[j : j + 1]
        asend[j, 1:2] = stats[j : j + 1]

    owner = lax.div(my_kv, 2)
    slot = (4 * g + my_row) * 2 + zh

    for a, b, e, k in OWNERS[:-1]:
        j = 4 * rem(x + a, 2) + rem(y + b, 4)
        device = (owner, (div(x, 2) * 8 + j) * 4 + 2 * rem(zh + e, 2) + rem(c + k, 2))
        remote(asend.at[j], arecv.at[slot], 7, device).start()

    @pl.when(owner != g)
    def _():
        remote(asend.at[rem(xy, 8)], arecv.at[slot], 7, (owner, t)).start()
        settle(arecv, recv_sem.at[7])

    @pl.when(owner == g)
    def _():
        arecv[slot] = asend[rem(xy, 8)]
        settle(arecv.at[pl.ds(0, 31)], recv_sem.at[7])

    for i in range(16):
        for side in range(2):
            hd[2 * side, i : i + 1] = arecv[2 * i + side, 0:1]
            hd[2 * side + 1, i : i + 1] = arecv[2 * i + side, 1:2]
    left, right = hd[1], hd[3]
    most = jnp.maximum(left[:, 0:1], right[:, 0:1])
    left_factor = jnp.exp(left[:, 0:1] - most)
    right_factor = jnp.exp(right[:, 0:1] - most)
    heads = (hd[0] * left_factor + hd[2] * right_factor) / (
        left[:, 64:65] * left_factor + right[:, 64:65] * right_factor
    )
    heads = jnp.where(zh == 1, pltpu.roll(heads, 64, 1), heads).astype(BF16)[:, :64]

    for tile in range(20):
        part = jnp.dot(
            heads, mo[:, 128 * tile : 128 * (tile + 1)], preferred_element_type=F32
        )
        for i in range(G):
            if tile < XY:
                bsend[tile, i] = part[4 * i : 4 * i + 4]
            else:
                bsend[4 * i + tile - XY, 4] = part[4 * i : 4 * i + 4]
    to_plane(lambda there: bsend.at[there], brecv.at[xy], 8)
    brecv[xy] = bsend[xy]
    settle(brecv.at[pl.ds(0, XY - 1)], recv_sem.at[8])
    total = jnp.sum(brecv[...], axis=0)
    for i in range(G):
        ysend[i, 0] = total[i]
        ysend[i, 1] = total[4]
    to_z(lambda group: ysend.at[group], yrecv.at[z], 9)
    yrecv[z] = ysend[g]
    settle(yrecv.at[pl.ds(0, 7)], recv_sem.at[9])
    osend[...] = jnp.sum(yrecv[...], axis=0).astype(BF16)
    whole = pl.ds(pl.multiple_of(c * (OW // 2) + xy * 128, 128), 128)
    rest = pl.ds(pl.multiple_of(c * (OW // 2) + 2048 + y * 128, 128), 128)

    def everyone():
        for a, b, k in PLANE_CORES[:-1]:
            yield (g, chip(a, b) * 4 + zh * 2 + rem(c + k, 2))

    @pl.when(x == g)
    def _():
        for device in everyone():
            remote(osend.at[0], out.at[:, whole], 10, device).start()
            remote(osend.at[1], out.at[:, rest], 10, device).start()
        copies = [
            pltpu.make_async_copy(osend.at[0], out.at[:, whole], load_sem.at[0]),
            pltpu.make_async_copy(osend.at[1], out.at[:, rest], load_sem.at[1]),
        ]
        for copy in copies:
            copy.start()
        for copy in copies:
            copy.wait()
        settle(out.at[:, pl.ds(0, 38 * 128)], recv_sem.at[10])

    @pl.when(x != g)
    def _():
        for device in everyone():
            remote(osend.at[0], out.at[:, whole], 10, device).start()
        copy = pltpu.make_async_copy(osend.at[0], out.at[:, whole], load_sem.at[0])
        copy.start()
        copy.wait()
        settle(out.at[:, pl.ds(0, 39 * 128)], recv_sem.at[10])

    for copy in swaps:
        copy.wait_send()
    for stage, ref, count in (
        (0, hrecv, 3), (1, ra, 15), (2, rb, 15), (3, qrecv, 15), (4, zrecv, 7), (5, keys, 31),
        (6, values, 31), (8, brecv, 15), (9, yrecv, 7), (11, krecv, 15), (12, nrecv, 7),
    ):
        settle(ref.at[pl.ds(0, count)], send_sem.at[stage])
    settle(out.at[:, pl.ds(0, 31 * 128)], send_sem.at[10])

    @pl.when(x == g)
    def _():
        settle(out.at[:, pl.ds(0, 31 * 128)], send_sem.at[10])

    settle(arecv.at[pl.ds(0, 31)], send_sem.at[7])


    @pl.when(owner != g)
    def _():
        settle(arecv.at[0], send_sem.at[7])


def shards(*args):
    hbm = pl.BlockSpec(memory_space=pltpu.HBM)
    f32 = lambda *shape: pltpu.VMEM(shape, F32)
    bf16 = lambda *shape: pltpu.VMEM(shape, BF16)
    return pl.pallas_call(
        kernel,
        out_shape=jax.ShapeDtypeStruct((R, OW), BF16),
        in_specs=[hbm] * 17,
        out_specs=hbm,
        scratch_shapes=[
            pltpu.SMEM((R,), jnp.int32), pltpu.SMEM((R,), jnp.int32),
            bf16(3, DEPTH, QW), bf16(3, DEPTH, KW), bf16(3, DEPTH, KW), bf16(3, ODEPTH, OW),
            bf16(3, DEPTH, QW // 2), bf16(3, DEPTH, KW // 2), bf16(3, DEPTH, KW // 2), bf16(3, ODEPTH, OW // 2),
            bf16(32, SPAN, HD), bf16(32, SPAN, HD), bf16(R, 5120),
            f32(G, R, HD), f32(G, R, HD), f32(16, HD),
            f32(1, HD), f32(XY, 1, HD), f32(1, HD), f32(16, 1, HD),
            bf16(64, QW // 2), bf16(64, KW), bf16(64, OW // 2),
            f32(4, G, R, 8, HD), f32(XY, G, 8, HD), f32(4, G, R, 2, HD), f32(XY, G, 2, HD),
            f32(G, 8, HD), f32(8, 8, HD), f32(G, 2, HD), f32(8, 2, HD),
            f32(8, 2, HD), f32(32, 2, HD), f32(4, 16, HD),
            f32(XY, 5, R, HD), f32(XY, 5, R, HD), f32(G, 2, R, HD), f32(8, 2, R, HD),
            bf16(2, R, HD),
            pltpu.SemaphoreType.DMA((17,)), pltpu.SemaphoreType.DMA((12,)), pltpu.SemaphoreType.DMA((12,)),
            pltpu.SemaphoreType.DMA((13,)), pltpu.SemaphoreType.DMA((13,)),
        ],
        compiler_params=pltpu.CompilerParams(
            collective_id=0, has_side_effects=True, vmem_limit_bytes=56 * 1024 * 1024
        ),
        cost_estimate=pl.CostEstimate(flops=40_000_000, bytes_accessed=4_000_000, transcendentals=100_000),
    )(*args)


def solution(mesh):
    both = P(("group", "tensor"), None)
    cache = P("group", None, "tensor", None)
    in_specs = (both,) * 12 + (P("group", None), cache, cache, P("group"), P("group"))
    return jax.shard_map(
        shards, mesh=mesh, in_specs=in_specs, out_specs=P("group", None), check_vma=False
    )
```

```python
import math

import jax
import jax.numpy as jnp
import numpy as np
from jax import lax
from jax.experimental import pallas as pl
from jax.experimental.pallas import tpu as pltpu
from jax.sharding import PartitionSpec as P

MESH = pl.DeviceIdType.MESH
F32 = jnp.float32
BF16 = jnp.bfloat16
G, XY, W = 4, 16, 4
R, HD, SPAN = 4, 128, 64
QW, KW, OW = 8192, 1024, 5120
DEPTH, ODEPTH = 20, 32
FREQ = (1000000.0 ** (-np.arange(HD // 2) / (HD // 2))).astype(np.float32)


def ring(step, size):
    return min(step, size - step)


PLANE = sorted(((a, b) for a in range(4) for b in range(4)), key=lambda s: -ring(s[0], 4) - ring(s[1], 4))
NEAR = PLANE[-2::-1] + PLANE[-1:]
PLANE_CORES = sorted(
    ((a, b, k) for a, b in PLANE for k in range(2)),
    key=lambda s: -ring(s[0], 4) - ring(s[1], 4) - 0.1 * s[2],
)
LINE = sorted(range(8), key=lambda s: -ring(s, 8))
COLUMN = sorted(((a, k) for a in LINE for k in range(2)), key=lambda s: -ring(s[0], 8) - 0.1 * s[1])
OWNERS = sorted(
    ((a, b, e, k) for a in range(2) for b in range(4) for e in range(2) for k in range(2)),
    key=lambda s: -s[0] - ring(s[1], 4) - 3 * s[2] - 0.1 * s[3],
)
SCALE = 1.0 / math.sqrt(HD)


def kernel(
    qi, qf, qs, ki, kf, ks, vi, vf, vs, oi, of, os_, hid, ck, cv, pos_in, lens_in,
    out,
    pos, lens,
    wq, wk, wv, wo, pq, pk, pv, po, keys, values, hv,
    hsend, hrecv, hfull, sa, ra, sb, rb, mq, mkv, mo,
    qsend, qrecv, ksend, krecv, zsend, zrecv, nsend, nrecv,
    asend, arecv, hd, bsend, brecv, ysend, yrecv, osend,
    load_sem, swap_send, swap_recv, send_sem, recv_sem,
):
    g = lax.axis_index("group")
    t = lax.axis_index("tensor")
    xy, w = lax.div(t, 4), lax.rem(t, 4)
    zh, c = lax.div(w, 2), lax.rem(w, 2)
    x, y = lax.div(xy, 4), lax.rem(xy, 4)
    z = zh * 4 + g
    my_row = 2 * lax.rem(x, 2) + lax.div(y, 2)
    my_kind = 2 * lax.rem(y, 2) + lax.div(x, 2)
    my_kv = 4 * c + my_kind

    def remote(src, dst, stage, device):
        return pltpu.make_async_remote_copy(
            src_ref=src, dst_ref=dst, send_sem=send_sem.at[stage], recv_sem=recv_sem.at[stage],
            device_id=device, device_id_type=MESH,
        )

    def settle(ref, sem):
        pltpu.make_async_copy(ref, ref, sem).wait()

    raw = [(qi, qf, qs), (ki, kf, ks), (vi, vf, vs), (oi, of, os_)]
    mine = [wq, wk, wv, wo]
    theirs = [pq, pk, pv, po]
    loads = []
    for m in range(4):
        for j in range(3):
            loads.append(pltpu.make_async_copy(raw[m][j], mine[m].at[j], load_sem.at[3 * m + j]))
    place = 2 * xy + c
    loads.append(pltpu.make_async_copy(ck.at[my_row, my_kv], keys.at[place], load_sem.at[12]))
    loads.append(pltpu.make_async_copy(cv.at[my_row, my_kv], values.at[place], load_sem.at[13]))
    loads.append(pltpu.make_async_copy(hid, hv, load_sem.at[14]))
    loads.append(pltpu.make_async_copy(pos_in, pos, load_sem.at[15]))
    loads.append(pltpu.make_async_copy(lens_in, lens, load_sem.at[16]))
    for copy in loads:
        copy.start()

    rem, div = lax.rem, lax.div

    def chip(a, b):
        return rem(x + a, 4) * 4 + rem(y + b, 4)

    def column(a, k):
        there = rem(z + a, 8)
        return (rem(there, 4), xy * 4 + div(there, 4) * 2 + rem(c + k, 2))

    barrier = pltpu.get_barrier_semaphore()
    for a, k in COLUMN[:-1]:
        pl.semaphore_signal(barrier, inc=1, device_id=column(a, k), device_id_type=MESH)
    for a, b in PLANE[:-1]:
        there = (g, chip(a, b) * 4 + w)
        pl.semaphore_signal(barrier, inc=1, device_id=there, device_id_type=MESH)

    loads[14].wait()
    place = 40 * (t // 2)
    base = jnp.minimum(place // 128, 8) * 128
    lane = lax.broadcasted_iota(jnp.int32, (256, 128), 1)
    row = lax.broadcasted_iota(jnp.int32, (256, 128), 0)
    piece, step = lane // 32, lane % 32
    wanted = place - base + step + 20 * jnp.where(piece == 0, c, 1 - c)
    pick = jnp.where((row == wanted) & (lane < 64) & (step < 20), 1.0, 0.0).astype(BF16)
    for to in range(G):
        window = hv[:, pl.ds(pl.multiple_of(1280 * to + base, 128), 256)]
        hsend[to] = jnp.dot(window, pick, preferred_element_type=F32)

    def sums(ref, rows, width, step):
        def body(i, acc):
            at = pl.ds(pl.multiple_of(i * step, step), step)
            init = ref[0, :, at].astype(F32)
            a = ref[1, :, at].astype(F32) - init
            b = ref[2, :, at].astype(F32) - init
            return (acc[0] + a * a, acc[1] + b * b, acc[2] + a * b)

        zero = jnp.zeros((rows, step), F32)
        totals = lax.fori_loop(0, width // step, body, (zero, zero, zero), unroll=2)
        done = []
        for total in totals:
            line = jnp.sum(total, axis=0, keepdims=True)
            done.append(sum(line[:, 128 * j : 128 * (j + 1)] for j in range(step // 128)))
        return done

    sub16 = lax.broadcasted_iota(jnp.int32, (16, 128), 0)
    lane16 = lax.broadcasted_iota(jnp.int32, (16, 128), 1)
    stack = jnp.zeros((16, 128), F32)
    for m, (ref, rows, width) in enumerate(
        ((wq, DEPTH, QW), (wk, DEPTH, KW), (wv, DEPTH, KW), (wo, ODEPTH, OW))
    ):
        for j in range(3):
            loads[3 * m + j].wait()
        for kind, line in enumerate(sums(ref, rows, width, 256)):
            stack = jnp.where(sub16 == 4 * kind + m, line, stack)
    stack = jnp.sum(stack, axis=1, keepdims=True)
    sa[...] = jnp.sum(jnp.where(sub16 == lane16, stack, 0.0), axis=0, keepdims=True)

    pl.semaphore_wait(barrier, 30)

    def to_plane(src, dst, stage):
        for a, b in PLANE[:-1]:
            there = chip(a, b)
            remote(src(there), dst, stage, (g, there * 4 + w)).start()

    to_plane(lambda there: sa, ra.at[xy], 1)
    ra[xy] = sa[...]

    other = (g, t + 1 - 2 * c)
    swaps = []
    for m, width in enumerate((QW // 2, KW // 2, KW // 2, OW // 2)):
        for j in range(3):
            start = pl.multiple_of((1 - c) * width, 128)
            swaps.append(
                pltpu.make_async_remote_copy(
                    src_ref=raw[m][j].at[:, pl.ds(start, width)], dst_ref=theirs[m].at[j],
                    send_sem=swap_send.at[3 * m + j], recv_sem=swap_recv.at[3 * m + j],
                    device_id=other, device_id_type=MESH,
                )
            )
    for i in range(1, G):
        to = rem(g + i, G)
        remote(hsend.at[to], hrecv.at[g], 0, (to, t)).start()
    hrecv[g] = hsend[g]
    for copy in swaps:
        copy.start()

    def send_cache(src, dst, stage, core, first, last):
        for a, b in NEAR[first:last]:
            to_x, to_y = rem(x + a, 4), rem(y + b, 4)
            row = 2 * rem(to_x, 2) + div(to_y, 2)
            kv = 4 * core + 2 * rem(to_y, 2) + div(to_x, 2)
            device = (g, (4 * to_x + to_y) * 4 + zh * 2 + core)
            remote(src.at[row, kv], dst.at[2 * xy + c], stage, device).start()

    send_cache(ck, keys, 5, c, 0, 15)
    send_cache(cv, values, 6, c, 0, 15)
    settle(ra.at[pl.ds(0, XY - 1)], recv_sem.at[1])
    sb[...] = jnp.sum(ra[...], axis=0)

    for a, k in COLUMN[:-1]:
        remote(sb, rb.at[g * 4 + w], 2, column(a, k)).start()
    rb[g * 4 + w] = sb[...]

    send_cache(ck, keys, 5, 1 - c, 0, 16)
    send_cache(cv, values, 6, 1 - c, 0, 8)
    mq[...] = jnp.zeros_like(mq)
    mkv[...] = jnp.zeros_like(mkv)
    settle(hrecv.at[pl.ds(0, G - 1)], recv_sem.at[0])
    for i in range(G):
        hfull[4 * i : 4 * i + 4, :] = hrecv[i]
    rows_all = hfull[...].astype(BF16)[:, :64]
    loads[15].wait()
    loads[16].wait()
    turn = lax.broadcasted_iota(jnp.int32, (8, HD), 1)
    freq = jnp.ones((8, HD), F32)
    for j, value in enumerate(FREQ):
        freq = jnp.where(turn % (HD // 2) == j, float(value), freq)
    angle = pos[my_row].astype(F32) * freq
    cosine = jnp.cos(angle)
    sine = jnp.sin(angle)
    sine = jnp.where(turn < HD // 2, -sine, sine)

    def rotate(value):
        return value * cosine + pltpu.roll(value, HD // 2, 1) * sine

    for copy in swaps:
        copy.wait_recv()

    settle(rb.at[pl.ds(0, 15)], recv_sem.at[2])
    total = jnp.broadcast_to(jnp.sum(rb[...], axis=0), (8, 128))
    bb = pltpu.roll(total, 124, 1)
    ab = pltpu.roll(total, 120, 1)
    similar = ab / jnp.sqrt(total * bb + 1e-06)
    share = 1.0 / jnp.sqrt(2.0 * (1.0 + similar))
    lane8 = lax.broadcasted_iota(jnp.int32, (8, 128), 1)
    shares = [
        jnp.sum(jnp.where(lane8 == m, share, 0.0), axis=1, keepdims=True)[0:1] for m in range(4)
    ]

    def merge(init, first, second, factor):
        base = init.astype(F32)
        a = first.astype(F32) - base
        b = second.astype(F32) - base
        return (base + factor * a + factor * b).astype(BF16)

    def merge_into(dst, offset, own, swapped, own_row, other_row, width, factor, step):
        def body(i, _):
            there = pl.ds(pl.multiple_of(i * step, step), step)
            here = pl.ds(pl.multiple_of(c * width + i * step, step), step)
            to = pl.ds(pl.multiple_of(offset + i * step, step), step)
            dst[own_row, to] = merge(own[0, :, here], own[1, :, here], own[2, :, here], factor)
            dst[other_row, to] = merge(
                swapped[0, :, there], swapped[1, :, there], swapped[2, :, there], factor
            )
            return 0

        lax.fori_loop(0, width // step, body, 0, unroll=2)

    top, bottom = pl.ds(0, DEPTH), pl.ds(32, DEPTH)
    merge_into(mq, 0, wq, pq, top, bottom, QW // 2, shares[0], 256)

    flat = qsend.reshape(4 * 16 * 8, HD)
    for kind in range(4):
        for half in range(2):
            start = 1024 * kind + 512 * half
            part = jnp.dot(rows_all, mq[:, start : start + 512], preferred_element_type=F32)
            for j in range(4):
                at = pl.ds(128 * kind + 4 * half + j, 16, stride=8)
                flat[at, :] = part[:, 128 * j : 128 * (j + 1)]

    def piece_for(there):
        return (2 * rem(there, 2) + div(there, 8), slice(None), div(rem(there, 8), 2))

    to_plane(lambda there: qsend.at[piece_for(there)], qrecv.at[xy], 3)
    qrecv[xy] = qsend[my_kind, :, my_row]

    merge_into(mkv, 0, wk, pk, top, bottom, KW // 2, shares[1], 256)
    merge_into(mkv, KW // 2, wv, pv, top, bottom, KW // 2, shares[2], 256)
    new = jnp.dot(rows_all, mkv[...], preferred_element_type=F32)
    flat_new = ksend.reshape(4 * 16 * 2, HD)
    for kind in range(4):
        for j in range(2):
            start = 512 * j + 128 * kind
            flat_new[pl.ds(32 * kind + j, 16, stride=2), :] = new[:, start : start + 128]
    to_plane(lambda there: ksend.at[piece_for(there)], krecv.at[xy], 11)
    krecv[xy] = ksend[my_kind, :, my_row]

    merge_into(
        mo, 0, wo, po, pl.ds(pl.multiple_of(32 * c, 32), 32),
        pl.ds(pl.multiple_of(32 * (1 - c), 32), 32), OW // 2, shares[3], 256,
    )

    def to_z(src, dst, stage):
        for a in LINE[:-1]:
            device = column(a, 0)
            remote(src(device[0]), dst, stage, device).start()

    settle(qrecv.at[pl.ds(0, XY - 1)], recv_sem.at[3])
    zsend[...] = jnp.sum(qrecv[...], axis=0)
    to_z(lambda group: zsend.at[group], zrecv.at[z], 4)
    zrecv[z] = zsend[g]
    send_cache(cv, values, 6, 1 - c, 8, 16)
    settle(krecv.at[pl.ds(0, XY - 1)], recv_sem.at[11])
    nsend[...] = jnp.sum(krecv[...], axis=0)
    to_z(lambda group: nsend.at[group], nrecv.at[z], 12)
    nrecv[z] = nsend[g]

    loads[12].wait()
    loads[13].wait()
    settle(keys.at[pl.ds(0, 31)], recv_sem.at[5])
    settle(values.at[pl.ds(0, 31)], recv_sem.at[6])
    settle(zrecv.at[pl.ds(0, 7)], recv_sem.at[4])
    query = rotate(jnp.sum(zrecv[...], axis=0)).astype(BF16)
    length = lens[my_row]
    lane = lax.broadcasted_iota(jnp.int32, (8, 128), 1)
    low = lane < SPAN
    scores, peaks = [], []
    for chunk in range(8):
        score = lax.dot_general(
            query, keys[4 * chunk : 4 * chunk + 4].reshape(4 * SPAN, HD),
            (((1,), (1,)), ((), ())), preferred_element_type=F32,
        )
        for i in range(2):
            slot = (4 * (2 * chunk + i) + 2 * zh) * SPAN + lane
            valid = slot < length
            part = jnp.where(valid, score[:, 128 * i : 128 * (i + 1)] * SCALE, -1e30)
            left = jnp.max(jnp.where(low, part, -1e30), axis=1, keepdims=True)
            right = jnp.max(jnp.where(low, -1e30, part), axis=1, keepdims=True)
            scores.append((part, valid))
            peaks.append(jnp.where(low, left, right))
    most = peaks[0]
    for peak in peaks[1:]:
        most = jnp.maximum(most, peak)
    most = jnp.maximum(most, pltpu.roll(most, 64, 1))
    mass = jnp.zeros((8, 128), F32)
    mixed = jnp.zeros((24, HD), F32)
    for chunk in range(8):
        terms = []
        for i in range(2):
            (part, valid), peak = scores[2 * chunk + i], peaks[2 * chunk + i]
            weight = jnp.where(valid, jnp.exp(part - peak), 0.0).astype(BF16).astype(F32)
            weight = weight * jnp.exp(peak - most)
            mass = mass + weight
            first = weight.astype(BF16)
            rest = weight - first.astype(F32)
            second = rest.astype(BF16)
            third = (rest - second.astype(F32)).astype(BF16)
            terms.append(jnp.concatenate([first, second, third], axis=0))
        mixed = mixed + jnp.dot(
            jnp.concatenate(terms, axis=1),
            values[4 * chunk : 4 * chunk + 4].reshape(4 * SPAN, HD),
            preferred_element_type=F32,
        )
    mixed = mixed[0:8] + mixed[8:16] + mixed[16:24]
    mass = jnp.sum(mass, axis=1, keepdims=True)
    most = most[:, 0:1]

    settle(nrecv.at[pl.ds(0, 7)], recv_sem.at[12])
    new = jnp.sum(nrecv[...], axis=0)
    new_key = jnp.broadcast_to(new[0:1], (8, HD))
    new_key = rotate(new_key).astype(BF16).astype(F32)
    new_value = new[1:2].astype(BF16).astype(F32)
    own = jnp.sum(query.astype(F32) * new_key, axis=1, keepdims=True) * SCALE
    own = jnp.where(zh == 0, own, most)
    peak = jnp.maximum(most, own)
    old = jnp.exp(most - peak)
    fresh = jnp.where(zh == 0, jnp.exp(own - peak), 0.0)
    mixed = mixed * old + fresh * new_value
    stats = jnp.where(low, peak, mass * old + fresh)
    for j in range(8):
        asend[j, 0:1] = mixed[j : j + 1]
        asend[j, 1:2] = stats[j : j + 1]

    owner = lax.div(my_kv, 2)
    slot = (4 * g + my_row) * 2 + zh

    for a, b, e, k in OWNERS[:-1]:
        j = 4 * rem(x + a, 2) + rem(y + b, 4)
        device = (owner, (div(x, 2) * 8 + j) * 4 + 2 * rem(zh + e, 2) + rem(c + k, 2))
        remote(asend.at[j], arecv.at[slot], 7, device).start()

    @pl.when(owner != g)
    def _():
        remote(asend.at[rem(xy, 8)], arecv.at[slot], 7, (owner, t)).start()
        settle(arecv, recv_sem.at[7])

    @pl.when(owner == g)
    def _():
        arecv[slot] = asend[rem(xy, 8)]
        settle(arecv.at[pl.ds(0, 31)], recv_sem.at[7])

    for i in range(16):
        for side in range(2):
            hd[2 * side, i : i + 1] = arecv[2 * i + side, 0:1]
            hd[2 * side + 1, i : i + 1] = arecv[2 * i + side, 1:2]
    left, right = hd[1], hd[3]
    most = jnp.maximum(left[:, 0:1], right[:, 0:1])
    left_factor = jnp.exp(left[:, 0:1] - most)
    right_factor = jnp.exp(right[:, 0:1] - most)
    heads = (hd[0] * left_factor + hd[2] * right_factor) / (
        left[:, 64:65] * left_factor + right[:, 64:65] * right_factor
    )
    heads = jnp.where(zh == 1, pltpu.roll(heads, 64, 1), heads).astype(BF16)[:, :64]

    for tile in range(20):
        part = jnp.dot(
            heads, mo[:, 128 * tile : 128 * (tile + 1)], preferred_element_type=F32
        )
        for i in range(G):
            if tile < XY:
                bsend[tile, i] = part[4 * i : 4 * i + 4]
            else:
                bsend[4 * i + tile - XY, 4] = part[4 * i : 4 * i + 4]
    to_plane(lambda there: bsend.at[there], brecv.at[xy], 8)
    brecv[xy] = bsend[xy]
    settle(brecv.at[pl.ds(0, XY - 1)], recv_sem.at[8])
    total = jnp.sum(brecv[...], axis=0)
    for i in range(G):
        ysend[i, 0] = total[i]
        ysend[i, 1] = total[4]
    to_z(lambda group: ysend.at[group], yrecv.at[z], 9)
    yrecv[z] = ysend[g]
    settle(yrecv.at[pl.ds(0, 7)], recv_sem.at[9])
    osend[...] = jnp.sum(yrecv[...], axis=0).astype(BF16)
    whole = pl.ds(pl.multiple_of(c * (OW // 2) + xy * 128, 128), 128)
    rest = pl.ds(pl.multiple_of(c * (OW // 2) + 2048 + y * 128, 128), 128)

    def everyone():
        for a, b, k in PLANE_CORES[:-1]:
            yield (g, chip(a, b) * 4 + zh * 2 + rem(c + k, 2))

    @pl.when(x == g)
    def _():
        for device in everyone():
            remote(osend.at[0], out.at[:, whole], 10, device).start()
            remote(osend.at[1], out.at[:, rest], 10, device).start()
        copies = [
            pltpu.make_async_copy(osend.at[0], out.at[:, whole], load_sem.at[0]),
            pltpu.make_async_copy(osend.at[1], out.at[:, rest], load_sem.at[1]),
        ]
        for copy in copies:
            copy.start()
        for copy in copies:
            copy.wait()
        settle(out.at[:, pl.ds(0, 38 * 128)], recv_sem.at[10])

    @pl.when(x != g)
    def _():
        for device in everyone():
            remote(osend.at[0], out.at[:, whole], 10, device).start()
        copy = pltpu.make_async_copy(osend.at[0], out.at[:, whole], load_sem.at[0])
        copy.start()
        copy.wait()
        settle(out.at[:, pl.ds(0, 39 * 128)], recv_sem.at[10])

    for copy in swaps:
        copy.wait_send()
    for stage, ref, count in (
        (0, hrecv, 3), (1, ra, 15), (2, rb, 15), (3, qrecv, 15), (4, zrecv, 7), (5, keys, 31),
        (6, values, 31), (8, brecv, 15), (9, yrecv, 7), (11, krecv, 15), (12, nrecv, 7),
    ):
        settle(ref.at[pl.ds(0, count)], send_sem.at[stage])
    settle(out.at[:, pl.ds(0, 31 * 128)], send_sem.at[10])

    @pl.when(x == g)
    def _():
        settle(out.at[:, pl.ds(0, 31 * 128)], send_sem.at[10])

    settle(arecv.at[pl.ds(0, 31)], send_sem.at[7])


    @pl.when(owner != g)
    def _():
        settle(arecv.at[0], send_sem.at[7])


def shards(*args):
    hbm = pl.BlockSpec(memory_space=pltpu.HBM)
    f32 = lambda *shape: pltpu.VMEM(shape, F32)
    bf16 = lambda *shape: pltpu.VMEM(shape, BF16)
    return pl.pallas_call(
        kernel,
        out_shape=pltpu.VMEM((R, OW), BF16),
        in_specs=[hbm] * 17,
        out_specs=pl.BlockSpec(memory_space=pl.ANY),
        scratch_shapes=[
            pltpu.SMEM((R,), jnp.int32), pltpu.SMEM((R,), jnp.int32),
            bf16(3, DEPTH, QW), bf16(3, DEPTH, KW), bf16(3, DEPTH, KW), bf16(3, ODEPTH, OW),
            bf16(3, DEPTH, QW // 2), bf16(3, DEPTH, KW // 2), bf16(3, DEPTH, KW // 2), bf16(3, ODEPTH, OW // 2),
            bf16(32, SPAN, HD), bf16(32, SPAN, HD), bf16(R, 5120),
            f32(G, R, HD), f32(G, R, HD), f32(16, HD),
            f32(1, HD), f32(XY, 1, HD), f32(1, HD), f32(16, 1, HD),
            bf16(64, QW // 2), bf16(64, KW), bf16(64, OW // 2),
            f32(4, G, R, 8, HD), f32(XY, G, 8, HD), f32(4, G, R, 2, HD), f32(XY, G, 2, HD),
            f32(G, 8, HD), f32(8, 8, HD), f32(G, 2, HD), f32(8, 2, HD),
            f32(8, 2, HD), f32(32, 2, HD), f32(4, 16, HD),
            f32(XY, 5, R, HD), f32(XY, 5, R, HD), f32(G, 2, R, HD), f32(8, 2, R, HD),
            bf16(2, R, HD),
            pltpu.SemaphoreType.DMA((17,)), pltpu.SemaphoreType.DMA((12,)), pltpu.SemaphoreType.DMA((12,)),
            pltpu.SemaphoreType.DMA((13,)), pltpu.SemaphoreType.DMA((13,)),
        ],
        compiler_params=pltpu.CompilerParams(
            collective_id=0, has_side_effects=True, vmem_limit_bytes=24 * 1024 * 1024
        ),
        cost_estimate=pl.CostEstimate(flops=40_000_000, bytes_accessed=4_000_000, transcendentals=100_000),
    )(*(pltpu.with_memory_space_constraint(arg, pltpu.HBM) for arg in args))


def solution(mesh):
    both = P(("group", "tensor"), None)
    cache = P("group", None, "tensor", None)
    in_specs = (both,) * 12 + (P("group", None), cache, cache, P("group"), P("group"))
    return jax.shard_map(
        shards, mesh=mesh, in_specs=in_specs, out_specs=P("group", None), check_vma=False
    )
```

```python
import math

import jax
import jax.numpy as jnp
import numpy as np
from jax import lax
from jax.experimental import pallas as pl
from jax.experimental.pallas import tpu as pltpu
from jax.sharding import PartitionSpec as P

MESH = pl.DeviceIdType.MESH
F32 = jnp.float32
BF16 = jnp.bfloat16
G, XY, W = 4, 16, 4
R, HD, SPAN = 4, 128, 64
QW, KW, OW = 8192, 1024, 5120
DEPTH, ODEPTH = 20, 32
FREQ = (1000000.0 ** (-np.arange(HD // 2) / (HD // 2))).astype(np.float32)


def ring(step, size):
    return min(step, size - step)


PLANE = sorted(((a, b) for a in range(4) for b in range(4)), key=lambda s: -ring(s[0], 4) - ring(s[1], 4))
NEAR = PLANE[-2::-1] + PLANE[-1:]
PLANE_CORES = sorted(
    ((a, b, k) for a, b in PLANE for k in range(2)),
    key=lambda s: -ring(s[0], 4) - ring(s[1], 4) - 0.1 * s[2],
)
LINE = sorted(range(8), key=lambda s: -ring(s, 8))
COLUMN = sorted(((a, k) for a in LINE for k in range(2)), key=lambda s: -ring(s[0], 8) - 0.1 * s[1])
OWNERS = sorted(
    ((a, b, e, k) for a in range(2) for b in range(4) for e in range(2) for k in range(2)),
    key=lambda s: -s[0] - ring(s[1], 4) - 3 * s[2] - 0.1 * s[3],
)
SCALE = 1.0 / math.sqrt(HD)


def kernel(
    qi, qf, qs, ki, kf, ks, vi, vf, vs, oi, of, os_, hid, ck, cv, pos_in, lens_in,
    out,
    pos, lens,
    wq, wk, wv, wo, pq, pk, pv, po, keys, values, hv,
    hsend, hrecv, hfull, sa, ra, sb, rb, mq, mkv, mo,
    qsend, qrecv, ksend, krecv, zsend, zrecv, nsend, nrecv,
    asend, arecv, hd, bsend, brecv, ysend, yrecv, osend,
    load_sem, swap_send, swap_recv, send_sem, recv_sem,
):
    g = lax.axis_index("group")
    t = lax.axis_index("tensor")
    xy, w = lax.div(t, 4), lax.rem(t, 4)
    zh, c = lax.div(w, 2), lax.rem(w, 2)
    x, y = lax.div(xy, 4), lax.rem(xy, 4)
    z = zh * 4 + g
    my_row = 2 * lax.rem(x, 2) + lax.div(y, 2)
    my_kind = 2 * lax.rem(y, 2) + lax.div(x, 2)
    my_kv = 4 * c + my_kind

    def remote(src, dst, stage, device):
        return pltpu.make_async_remote_copy(
            src_ref=src, dst_ref=dst, send_sem=send_sem.at[stage], recv_sem=recv_sem.at[stage],
            device_id=device, device_id_type=MESH,
        )

    def settle(ref, sem):
        pltpu.make_async_copy(ref, ref, sem).wait()

    raw = [(qi, qf, qs), (ki, kf, ks), (vi, vf, vs), (oi, of, os_)]
    mine = [wq, wk, wv, wo]
    theirs = [pq, pk, pv, po]
    loads = []
    for m in range(4):
        for j in range(3):
            loads.append(pltpu.make_async_copy(raw[m][j], mine[m].at[j], load_sem.at[3 * m + j]))
    place = 2 * xy + c
    loads.append(pltpu.make_async_copy(ck.at[my_row, my_kv], keys.at[place], load_sem.at[12]))
    loads.append(pltpu.make_async_copy(cv.at[my_row, my_kv], values.at[place], load_sem.at[13]))
    loads.append(pltpu.make_async_copy(hid, hv, load_sem.at[14]))
    loads.append(pltpu.make_async_copy(pos_in, pos, load_sem.at[15]))
    loads.append(pltpu.make_async_copy(lens_in, lens, load_sem.at[16]))
    for copy in loads:
        copy.start()

    rem, div = lax.rem, lax.div

    def chip(a, b):
        return rem(x + a, 4) * 4 + rem(y + b, 4)

    def column(a, k):
        there = rem(z + a, 8)
        return (rem(there, 4), xy * 4 + div(there, 4) * 2 + rem(c + k, 2))

    barrier = pltpu.get_barrier_semaphore()
    for a, k in COLUMN[:-1]:
        pl.semaphore_signal(barrier, inc=1, device_id=column(a, k), device_id_type=MESH)
    for a, b in PLANE[:-1]:
        there = (g, chip(a, b) * 4 + w)
        pl.semaphore_signal(barrier, inc=1, device_id=there, device_id_type=MESH)

    loads[14].wait()
    place = 40 * (t // 2)
    base = jnp.minimum(place // 128, 8) * 128
    lane = lax.broadcasted_iota(jnp.int32, (256, 128), 1)
    row = lax.broadcasted_iota(jnp.int32, (256, 128), 0)
    piece, step = lane // 32, lane % 32
    wanted = place - base + step + 20 * jnp.where(piece == 0, c, 1 - c)
    pick = jnp.where((row == wanted) & (lane < 64) & (step < 20), 1.0, 0.0).astype(BF16)
    for to in range(G):
        window = hv[:, pl.ds(pl.multiple_of(1280 * to + base, 128), 256)]
        hsend[to] = jnp.dot(window, pick, preferred_element_type=F32)

    def sums(ref, rows, width, step):
        def body(i, acc):
            at = pl.ds(pl.multiple_of(i * step, step), step)
            init = ref[0, :, at].astype(F32)
            a = ref[1, :, at].astype(F32) - init
            b = ref[2, :, at].astype(F32) - init
            return (acc[0] + a * a, acc[1] + b * b, acc[2] + a * b)

        zero = jnp.zeros((rows, step), F32)
        totals = lax.fori_loop(0, width // step, body, (zero, zero, zero), unroll=2)
        done = []
        for total in totals:
            line = jnp.sum(total, axis=0, keepdims=True)
            done.append(sum(line[:, 128 * j : 128 * (j + 1)] for j in range(step // 128)))
        return done

    sub16 = lax.broadcasted_iota(jnp.int32, (16, 128), 0)
    lane16 = lax.broadcasted_iota(jnp.int32, (16, 128), 1)
    stack = jnp.zeros((16, 128), F32)
    for m, (ref, rows, width) in enumerate(
        ((wq, DEPTH, QW), (wk, DEPTH, KW), (wv, DEPTH, KW), (wo, ODEPTH, OW))
    ):
        for j in range(3):
            loads[3 * m + j].wait()
        for kind, line in enumerate(sums(ref, rows, width, 256)):
            stack = jnp.where(sub16 == 4 * kind + m, line, stack)
    stack = jnp.sum(stack, axis=1, keepdims=True)
    sa[...] = jnp.sum(jnp.where(sub16 == lane16, stack, 0.0), axis=0, keepdims=True)

    pl.semaphore_wait(barrier, 30)

    def to_plane(src, dst, stage):
        for a, b in PLANE[:-1]:
            there = chip(a, b)
            remote(src(there), dst, stage, (g, there * 4 + w)).start()

    to_plane(lambda there: sa, ra.at[xy], 1)
    ra[xy] = sa[...]

    other = (g, t + 1 - 2 * c)
    swaps = []
    for m, width in enumerate((QW // 2, KW // 2, KW // 2, OW // 2)):
        for j in range(3):
            start = pl.multiple_of((1 - c) * width, 128)
            swaps.append(
                pltpu.make_async_remote_copy(
                    src_ref=raw[m][j].at[:, pl.ds(start, width)], dst_ref=theirs[m].at[j],
                    send_sem=swap_send.at[3 * m + j], recv_sem=swap_recv.at[3 * m + j],
                    device_id=other, device_id_type=MESH,
                )
            )
    for i in range(1, G):
        to = rem(g + i, G)
        remote(hsend.at[to], hrecv.at[g], 0, (to, t)).start()
    hrecv[g] = hsend[g]
    for copy in swaps:
        copy.start()

    def send_cache(src, dst, stage, core, first, last):
        for a, b in NEAR[first:last]:
            to_x, to_y = rem(x + a, 4), rem(y + b, 4)
            row = 2 * rem(to_x, 2) + div(to_y, 2)
            kv = 4 * core + 2 * rem(to_y, 2) + div(to_x, 2)
            device = (g, (4 * to_x + to_y) * 4 + zh * 2 + core)
            remote(src.at[row, kv], dst.at[2 * xy + c], stage, device).start()

    send_cache(ck, keys, 5, c, 0, 15)
    send_cache(cv, values, 6, c, 0, 15)
    settle(ra.at[pl.ds(0, XY - 1)], recv_sem.at[1])
    sb[...] = jnp.sum(ra[...], axis=0)

    for a, k in COLUMN[:-1]:
        remote(sb, rb.at[g * 4 + w], 2, column(a, k)).start()
    rb[g * 4 + w] = sb[...]

    send_cache(ck, keys, 5, 1 - c, 0, 16)
    send_cache(cv, values, 6, 1 - c, 0, 8)
    mq[...] = jnp.zeros_like(mq)
    mkv[...] = jnp.zeros_like(mkv)
    settle(hrecv.at[pl.ds(0, G - 1)], recv_sem.at[0])
    for i in range(G):
        hfull[4 * i : 4 * i + 4, :] = hrecv[i]
    rows_all = hfull[...].astype(BF16)[:, :64]
    loads[15].wait()
    loads[16].wait()
    turn = lax.broadcasted_iota(jnp.int32, (8, HD), 1)
    freq = jnp.ones((8, HD), F32)
    for j, value in enumerate(FREQ):
        freq = jnp.where(turn % (HD // 2) == j, float(value), freq)
    angle = pos[my_row].astype(F32) * freq
    cosine = jnp.cos(angle)
    sine = jnp.sin(angle)
    sine = jnp.where(turn < HD // 2, -sine, sine)

    def rotate(value):
        return value * cosine + pltpu.roll(value, HD // 2, 1) * sine

    for copy in swaps:
        copy.wait_recv()

    settle(rb.at[pl.ds(0, 15)], recv_sem.at[2])
    total = jnp.broadcast_to(jnp.sum(rb[...], axis=0), (8, 128))
    bb = pltpu.roll(total, 124, 1)
    ab = pltpu.roll(total, 120, 1)
    similar = ab / jnp.sqrt(total * bb + 1e-06)
    share = 1.0 / jnp.sqrt(2.0 * (1.0 + similar))
    lane8 = lax.broadcasted_iota(jnp.int32, (8, 128), 1)
    shares = [
        share[0:1, m : m + 1] for m in range(4)
    ]

    def merge(init, first, second, factor):
        base = init.astype(F32)
        a = first.astype(F32) - base
        b = second.astype(F32) - base
        return (base + factor * a + factor * b).astype(BF16)

    def merge_into(dst, offset, own, swapped, own_row, other_row, width, factor, step):
        def body(i, _):
            there = pl.ds(pl.multiple_of(i * step, step), step)
            here = pl.ds(pl.multiple_of(c * width + i * step, step), step)
            to = pl.ds(pl.multiple_of(offset + i * step, step), step)
            dst[own_row, to] = merge(own[0, :, here], own[1, :, here], own[2, :, here], factor)
            dst[other_row, to] = merge(
                swapped[0, :, there], swapped[1, :, there], swapped[2, :, there], factor
            )
            return 0

        lax.fori_loop(0, width // step, body, 0, unroll=8 if width > 2560 else 2)

    top, bottom = pl.ds(0, DEPTH), pl.ds(32, DEPTH)
    merge_into(mq, 0, wq, pq, top, bottom, QW // 2, shares[0], 256)

    flat = qsend.reshape(4 * 16 * 8, HD)
    for kind in range(4):
        part = jnp.dot(
            rows_all, mq[:, 1024 * kind : 1024 * (kind + 1)], preferred_element_type=F32
        )
        for j in range(8):
            flat[pl.ds(128 * kind + j, 16, stride=8), :] = part[:, 128 * j : 128 * (j + 1)]

    def piece_for(there):
        return (2 * rem(there, 2) + div(there, 8), slice(None), div(rem(there, 8), 2))

    to_plane(lambda there: qsend.at[piece_for(there)], qrecv.at[xy], 3)
    qrecv[xy] = qsend[my_kind, :, my_row]

    merge_into(mkv, 0, wk, pk, top, bottom, KW // 2, shares[1], 256)
    merge_into(mkv, KW // 2, wv, pv, top, bottom, KW // 2, shares[2], 256)
    new = jnp.dot(rows_all, mkv[...], preferred_element_type=F32)
    flat_new = ksend.reshape(4 * 16 * 2, HD)
    for kind in range(4):
        for j in range(2):
            start = 512 * j + 128 * kind
            flat_new[pl.ds(32 * kind + j, 16, stride=2), :] = new[:, start : start + 128]
    to_plane(lambda there: ksend.at[piece_for(there)], krecv.at[xy], 11)
    krecv[xy] = ksend[my_kind, :, my_row]

    merge_into(
        mo, 0, wo, po, pl.ds(pl.multiple_of(32 * c, 32), 32),
        pl.ds(pl.multiple_of(32 * (1 - c), 32), 32), OW // 2, shares[3], 256,
    )

    def to_z(src, dst, stage):
        for a in LINE[:-1]:
            device = column(a, 0)
            remote(src(device[0]), dst, stage, device).start()

    settle(qrecv.at[pl.ds(0, XY - 1)], recv_sem.at[3])
    zsend[...] = jnp.sum(qrecv[...], axis=0)
    to_z(lambda group: zsend.at[group], zrecv.at[z], 4)
    zrecv[z] = zsend[g]
    send_cache(cv, values, 6, 1 - c, 8, 16)
    settle(krecv.at[pl.ds(0, XY - 1)], recv_sem.at[11])
    nsend[...] = jnp.sum(krecv[...], axis=0)
    to_z(lambda group: nsend.at[group], nrecv.at[z], 12)
    nrecv[z] = nsend[g]

    loads[12].wait()
    loads[13].wait()
    settle(keys.at[pl.ds(0, 31)], recv_sem.at[5])
    settle(values.at[pl.ds(0, 31)], recv_sem.at[6])
    settle(zrecv.at[pl.ds(0, 7)], recv_sem.at[4])
    query = rotate(jnp.sum(zrecv[...], axis=0)).astype(BF16)
    length = lens[my_row]
    lane = lax.broadcasted_iota(jnp.int32, (8, 128), 1)
    low = lane < SPAN
    scores, peaks = [], []
    for chunk in range(8):
        score = lax.dot_general(
            query, keys[4 * chunk : 4 * chunk + 4].reshape(4 * SPAN, HD),
            (((1,), (1,)), ((), ())), preferred_element_type=F32,
        )
        for i in range(2):
            slot = (4 * (2 * chunk + i) + 2 * zh) * SPAN + lane
            valid = slot < length
            part = jnp.where(valid, score[:, 128 * i : 128 * (i + 1)] * SCALE, -1e30)
            left = jnp.max(jnp.where(low, part, -1e30), axis=1, keepdims=True)
            right = jnp.max(jnp.where(low, -1e30, part), axis=1, keepdims=True)
            scores.append((part, valid))
            peaks.append(jnp.where(low, left, right))
    most = peaks[0]
    for peak in peaks[1:]:
        most = jnp.maximum(most, peak)
    most = jnp.maximum(most, pltpu.roll(most, 64, 1))
    mass = jnp.zeros((8, 128), F32)
    mixed = jnp.zeros((24, HD), F32)
    for chunk in range(8):
        terms = []
        for i in range(2):
            (part, valid), peak = scores[2 * chunk + i], peaks[2 * chunk + i]
            weight = jnp.where(valid, jnp.exp(part - peak), 0.0).astype(BF16).astype(F32)
            weight = weight * jnp.exp(peak - most)
            mass = mass + weight
            first = weight.astype(BF16)
            rest = weight - first.astype(F32)
            second = rest.astype(BF16)
            third = (rest - second.astype(F32)).astype(BF16)
            terms.append(jnp.concatenate([first, second, third], axis=0))
        mixed = mixed + jnp.dot(
            jnp.concatenate(terms, axis=1),
            values[4 * chunk : 4 * chunk + 4].reshape(4 * SPAN, HD),
            preferred_element_type=F32,
        )
    mixed = mixed[0:8] + mixed[8:16] + mixed[16:24]
    mass = jnp.sum(mass, axis=1, keepdims=True)
    most = most[:, 0:1]

    settle(nrecv.at[pl.ds(0, 7)], recv_sem.at[12])
    new = jnp.sum(nrecv[...], axis=0)
    new_key = jnp.broadcast_to(new[0:1], (8, HD))
    new_key = rotate(new_key).astype(BF16).astype(F32)
    new_value = new[1:2].astype(BF16).astype(F32)
    own = jnp.sum(query.astype(F32) * new_key, axis=1, keepdims=True) * SCALE
    own = jnp.where(zh == 0, own, most)
    peak = jnp.maximum(most, own)
    old = jnp.exp(most - peak)
    fresh = jnp.where(zh == 0, jnp.exp(own - peak), 0.0)
    mixed = mixed * old + fresh * new_value
    stats = jnp.where(low, peak, mass * old + fresh)
    for j in range(8):
        asend[j, 0:1] = mixed[j : j + 1]
        asend[j, 1:2] = stats[j : j + 1]

    owner = lax.div(my_kv, 2)
    slot = (4 * g + my_row) * 2 + zh

    for a, b, e, k in OWNERS[:-1]:
        j = 4 * rem(x + a, 2) + rem(y + b, 4)
        device = (owner, (div(x, 2) * 8 + j) * 4 + 2 * rem(zh + e, 2) + rem(c + k, 2))
        remote(asend.at[j], arecv.at[slot], 7, device).start()

    @pl.when(owner != g)
    def _():
        remote(asend.at[rem(xy, 8)], arecv.at[slot], 7, (owner, t)).start()
        settle(arecv, recv_sem.at[7])

    @pl.when(owner == g)
    def _():
        arecv[slot] = asend[rem(xy, 8)]
        settle(arecv.at[pl.ds(0, 31)], recv_sem.at[7])

    for i in range(16):
        for side in range(2):
            hd[2 * side, i : i + 1] = arecv[2 * i + side, 0:1]
            hd[2 * side + 1, i : i + 1] = arecv[2 * i + side, 1:2]
    left, right = hd[1], hd[3]
    most = jnp.maximum(left[:, 0:1], right[:, 0:1])
    left_factor = jnp.exp(left[:, 0:1] - most)
    right_factor = jnp.exp(right[:, 0:1] - most)
    heads = (hd[0] * left_factor + hd[2] * right_factor) / (
        left[:, 64:65] * left_factor + right[:, 64:65] * right_factor
    )
    heads = jnp.where(zh == 1, pltpu.roll(heads, 64, 1), heads).astype(BF16)[:, :64]

    for tile in range(20):
        part = jnp.dot(
            heads, mo[:, 128 * tile : 128 * (tile + 1)], preferred_element_type=F32
        )
        for i in range(G):
            others = [4 * a + b for a in range(4) if a != i for b in range(4)]
            if tile >= 8:
                to, at = others[tile - 8], i
            else:
                to, at = 4 * i + tile // 2, (i, 4)[tile % 2]
            bsend[to, at] = part[4 * i : 4 * i + 4]
    to_plane(lambda there: bsend.at[there], brecv.at[xy], 8)
    brecv[xy] = bsend[xy]
    settle(brecv.at[pl.ds(0, XY - 1)], recv_sem.at[8])
    total = jnp.sum(brecv[...], axis=0)
    for i in range(G):
        ysend[i, 0] = total[i]
        ysend[i, 1] = total[4]
    to_z(lambda group: ysend.at[group], yrecv.at[z], 9)
    yrecv[z] = ysend[g]
    settle(yrecv.at[pl.ds(0, 7)], recv_sem.at[9])
    done = jnp.sum(yrecv[...], axis=0).astype(BF16)
    osend[:, 0:128] = done[0]
    osend[:, 128:256] = done[1]

    def finish(start, tiles):
        src = osend.at[:, pl.ds(0, 128 * tiles)]
        dst = out.at[:, pl.ds(pl.multiple_of(c * (OW // 2) + start, 128), 128 * tiles)]
        for a, b, k in PLANE_CORES[:-1]:
            device = (g, chip(a, b) * 4 + zh * 2 + rem(c + k, 2))
            remote(src, dst, 10, device).start()
        copy = pltpu.make_async_copy(src, dst, load_sem.at[0])
        copy.start()
        copy.wait()
        settle(out.at[:, pl.ds(0, (40 - tiles) * 128)], recv_sem.at[10])

    @pl.when(x == g)
    def _():
        finish(256 * y, 2)

    @pl.when(x < g)
    def _():
        finish(1024 + 128 * xy, 1)

    @pl.when(x > g)
    def _():
        finish(512 + 128 * xy, 1)

    for copy in swaps:
        copy.wait_send()
    for stage, ref, count in (
        (0, hrecv, 3), (1, ra, 15), (2, rb, 15), (3, qrecv, 15), (4, zrecv, 7), (5, keys, 31),
        (6, values, 31), (8, brecv, 15), (9, yrecv, 7), (11, krecv, 15), (12, nrecv, 7),
    ):
        settle(ref.at[pl.ds(0, count)], send_sem.at[stage])
    settle(out.at[:, pl.ds(0, 31 * 128)], send_sem.at[10])

    @pl.when(x == g)
    def _():
        settle(out.at[:, pl.ds(0, 31 * 128)], send_sem.at[10])

    settle(arecv.at[pl.ds(0, 31)], send_sem.at[7])


    @pl.when(owner != g)
    def _():
        settle(arecv.at[0], send_sem.at[7])


def shards(*args):
    hbm = pl.BlockSpec(memory_space=pltpu.HBM)
    f32 = lambda *shape: pltpu.VMEM(shape, F32)
    bf16 = lambda *shape: pltpu.VMEM(shape, BF16)
    return pl.pallas_call(
        kernel,
        out_shape=pltpu.VMEM((R, OW), BF16),
        in_specs=[hbm] * 17,
        out_specs=pl.BlockSpec(memory_space=pl.ANY),
        scratch_shapes=[
            pltpu.SMEM((R,), jnp.int32), pltpu.SMEM((R,), jnp.int32),
            bf16(3, DEPTH, QW), bf16(3, DEPTH, KW), bf16(3, DEPTH, KW), bf16(3, ODEPTH, OW),
            bf16(3, DEPTH, QW // 2), bf16(3, DEPTH, KW // 2), bf16(3, DEPTH, KW // 2), bf16(3, ODEPTH, OW // 2),
            bf16(32, SPAN, HD), bf16(32, SPAN, HD), bf16(R, 5120),
            f32(G, R, HD), f32(G, R, HD), f32(16, HD),
            f32(1, HD), f32(XY, 1, HD), f32(1, HD), f32(16, 1, HD),
            bf16(64, QW // 2), bf16(64, KW), bf16(64, OW // 2),
            f32(4, G, R, 8, HD), f32(XY, G, 8, HD), f32(4, G, R, 2, HD), f32(XY, G, 2, HD),
            f32(G, 8, HD), f32(8, 8, HD), f32(G, 2, HD), f32(8, 2, HD),
            f32(8, 2, HD), f32(32, 2, HD), f32(4, 16, HD),
            f32(XY, 5, R, HD), f32(XY, 5, R, HD), f32(G, 2, R, HD), f32(8, 2, R, HD),
            bf16(R, 2 * HD),
            pltpu.SemaphoreType.DMA((17,)), pltpu.SemaphoreType.DMA((12,)), pltpu.SemaphoreType.DMA((12,)),
            pltpu.SemaphoreType.DMA((13,)), pltpu.SemaphoreType.DMA((13,)),
        ],
        compiler_params=pltpu.CompilerParams(
            collective_id=0, has_side_effects=True, vmem_limit_bytes=24 * 1024 * 1024
        ),
        cost_estimate=pl.CostEstimate(flops=40_000_000, bytes_accessed=4_000_000, transcendentals=100_000),
    )(*(pltpu.with_memory_space_constraint(arg, pltpu.HBM) for arg in args))


def solution(mesh):
    both = P(("group", "tensor"), None)
    cache = P("group", None, "tensor", None)
    in_specs = (both,) * 12 + (P("group", None), cache, cache, P("group"), P("group"))
    return jax.shard_map(
        shards, mesh=mesh, in_specs=in_specs, out_specs=P("group", None), check_vma=False
    )
```

```python
import math

import jax
import jax.numpy as jnp
import numpy as np
from jax import lax
from jax.experimental import pallas as pl
from jax.experimental.pallas import tpu as pltpu
from jax.sharding import PartitionSpec as P

MESH = pl.DeviceIdType.MESH
F32 = jnp.float32
BF16 = jnp.bfloat16
G, XY, W = 4, 16, 4
R, HD, SPAN = 4, 128, 64
QW, KW, OW = 8192, 1024, 5120
DEPTH, ODEPTH = 20, 32
FREQ = (1000000.0 ** (-np.arange(HD // 2) / (HD // 2))).astype(np.float32)


def ring(step, size):
    return min(step, size - step)


PLANE = sorted(((a, b) for a in range(4) for b in range(4)), key=lambda s: -ring(s[0], 4) - ring(s[1], 4))
NEAR = PLANE[-2::-1] + PLANE[-1:]
PLANE_CORES = sorted(
    ((a, b, k) for a, b in PLANE for k in range(2)),
    key=lambda s: -ring(s[0], 4) - ring(s[1], 4) - 0.1 * s[2],
)
LINE = sorted(range(8), key=lambda s: -ring(s, 8))
COLUMN = sorted(((a, k) for a in LINE for k in range(2)), key=lambda s: -ring(s[0], 8) - 0.1 * s[1])
OWNERS = sorted(
    ((a, b, e, k) for a in range(2) for b in range(4) for e in range(2) for k in range(2)),
    key=lambda s: -s[0] - ring(s[1], 4) - 3 * s[2] - 0.1 * s[3],
)
SCALE = 1.0 / math.sqrt(HD)


def kernel(
    qi, qf, qs, ki, kf, ks, vi, vf, vs, oi, of, os_, hid, ck, cv, pos_in, lens_in,
    out,
    pos, lens,
    wq, wk, wv, wo, pq, pk, pv, po, keys, values, hv,
    hsend, hrecv, hfull, sa, ra, sb, rb, mq, mkv, mo,
    qsend, qrecv, ksend, krecv, zsend, zrecv, nsend, nrecv,
    asend, arecv, hd, bsend, brecv, ysend, yrecv, osend,
    load_sem, swap_send, swap_recv, send_sem, recv_sem,
):
    g = lax.axis_index("group")
    t = lax.axis_index("tensor")
    xy, w = lax.div(t, 4), lax.rem(t, 4)
    zh, c = lax.div(w, 2), lax.rem(w, 2)
    x, y = lax.div(xy, 4), lax.rem(xy, 4)
    z = zh * 4 + g
    my_row = 2 * lax.rem(x, 2) + lax.div(y, 2)
    my_kind = 2 * lax.rem(y, 2) + lax.div(x, 2)
    my_kv = 4 * c + my_kind

    def remote(src, dst, stage, device):
        return pltpu.make_async_remote_copy(
            src_ref=src, dst_ref=dst, send_sem=send_sem.at[stage], recv_sem=recv_sem.at[stage],
            device_id=device, device_id_type=MESH,
        )

    def settle(ref, sem):
        pltpu.make_async_copy(ref, ref, sem).wait()

    raw = [(qi, qf, qs), (ki, kf, ks), (vi, vf, vs), (oi, of, os_)]
    mine = [wq, wk, wv, wo]
    theirs = [pq, pk, pv, po]
    loads = []
    for m in range(4):
        for j in range(3):
            loads.append(pltpu.make_async_copy(raw[m][j], mine[m].at[j], load_sem.at[3 * m + j]))
    place = 2 * xy + c
    loads.append(pltpu.make_async_copy(ck.at[my_row, my_kv], keys.at[place], load_sem.at[12]))
    loads.append(pltpu.make_async_copy(cv.at[my_row, my_kv], values.at[place], load_sem.at[13]))
    loads.append(pltpu.make_async_copy(hid, hv, load_sem.at[14]))
    loads.append(pltpu.make_async_copy(pos_in, pos, load_sem.at[15]))
    loads.append(pltpu.make_async_copy(lens_in, lens, load_sem.at[16]))
    for copy in loads:
        copy.start()

    rem, div = lax.rem, lax.div

    def chip(a, b):
        return rem(x + a, 4) * 4 + rem(y + b, 4)

    def column(a, k):
        there = rem(z + a, 8)
        return (rem(there, 4), xy * 4 + div(there, 4) * 2 + rem(c + k, 2))

    barrier = pltpu.get_barrier_semaphore()
    for a, k in COLUMN[:-1]:
        pl.semaphore_signal(barrier, inc=1, device_id=column(a, k), device_id_type=MESH)
    for a, b in PLANE[:-1]:
        there = (g, chip(a, b) * 4 + w)
        pl.semaphore_signal(barrier, inc=1, device_id=there, device_id_type=MESH)

    loads[14].wait()
    place = 40 * (t // 2)
    base = jnp.minimum(place // 128, 8) * 128
    lane = lax.broadcasted_iota(jnp.int32, (256, 128), 1)
    row = lax.broadcasted_iota(jnp.int32, (256, 128), 0)
    piece, step = lane // 32, lane % 32
    wanted = place - base + step + 20 * jnp.where(piece == 0, c, 1 - c)
    pick = jnp.where((row == wanted) & (lane < 64) & (step < 20), 1.0, 0.0).astype(BF16)
    for to in range(G):
        window = hv[:, pl.ds(pl.multiple_of(1280 * to + base, 128), 256)]
        hsend[to] = jnp.dot(window, pick, preferred_element_type=F32)

    def sums(ref, rows, width, step):
        def body(i, acc):
            at = pl.ds(pl.multiple_of(i * step, step), step)
            init = ref[0, :, at].astype(F32)
            a = ref[1, :, at].astype(F32) - init
            b = ref[2, :, at].astype(F32) - init
            return (acc[0] + a * a, acc[1] + b * b, acc[2] + a * b)

        zero = jnp.zeros((rows, step), F32)
        totals = lax.fori_loop(0, width // step, body, (zero, zero, zero), unroll=2)
        done = []
        for total in totals:
            line = jnp.sum(total, axis=0, keepdims=True)
            done.append(sum(line[:, 128 * j : 128 * (j + 1)] for j in range(step // 128)))
        return done

    sub16 = lax.broadcasted_iota(jnp.int32, (16, 128), 0)
    lane16 = lax.broadcasted_iota(jnp.int32, (16, 128), 1)
    stack = jnp.zeros((16, 128), F32)
    for m, (ref, rows, width) in enumerate(
        ((wq, DEPTH, QW), (wk, DEPTH, KW), (wv, DEPTH, KW), (wo, ODEPTH, OW))
    ):
        for j in range(3):
            loads[3 * m + j].wait()
        for kind, line in enumerate(sums(ref, rows, width, 256)):
            stack = jnp.where(sub16 == 4 * kind + m, line, stack)
    stack = jnp.sum(stack, axis=1, keepdims=True)
    sa[...] = jnp.sum(jnp.where(sub16 == lane16, stack, 0.0), axis=0, keepdims=True)

    pl.semaphore_wait(barrier, 30)

    def to_plane(src, dst, stage):
        for a, b in PLANE[:-1]:
            there = chip(a, b)
            remote(src(there), dst, stage, (g, there * 4 + w)).start()

    to_plane(lambda there: sa, ra.at[xy], 1)
    ra[xy] = sa[...]

    other = (g, t + 1 - 2 * c)
    swaps = []
    for m, width in enumerate((QW // 2, KW // 2, KW // 2, OW // 2)):
        for j in range(3):
            start = pl.multiple_of((1 - c) * width, 128)
            swaps.append(
                pltpu.make_async_remote_copy(
                    src_ref=raw[m][j].at[:, pl.ds(start, width)], dst_ref=theirs[m].at[j],
                    send_sem=swap_send.at[3 * m + j], recv_sem=swap_recv.at[3 * m + j],
                    device_id=other, device_id_type=MESH,
                )
            )
    for i in range(1, G):
        to = rem(g + i, G)
        remote(hsend.at[to], hrecv.at[g], 0, (to, t)).start()
    hrecv[g] = hsend[g]
    for copy in swaps:
        copy.start()

    def send_cache(src, dst, stage, core, first, last):
        for a, b in NEAR[first:last]:
            to_x, to_y = rem(x + a, 4), rem(y + b, 4)
            row = 2 * rem(to_x, 2) + div(to_y, 2)
            kv = 4 * core + 2 * rem(to_y, 2) + div(to_x, 2)
            device = (g, (4 * to_x + to_y) * 4 + zh * 2 + core)
            remote(src.at[row, kv], dst.at[2 * xy + c], stage, device).start()

    send_cache(ck, keys, 5, c, 0, 15)
    send_cache(cv, values, 6, c, 0, 15)
    settle(ra.at[pl.ds(0, XY - 1)], recv_sem.at[1])
    sb[...] = jnp.sum(ra[...], axis=0)

    for a, k in COLUMN[:-1]:
        remote(sb, rb.at[g * 4 + w], 2, column(a, k)).start()
    rb[g * 4 + w] = sb[...]

    send_cache(ck, keys, 5, 1 - c, 0, 16)
    send_cache(cv, values, 6, 1 - c, 0, 8)
    mq[...] = jnp.zeros_like(mq)
    mkv[...] = jnp.zeros_like(mkv)
    settle(hrecv.at[pl.ds(0, G - 1)], recv_sem.at[0])
    for i in range(G):
        hfull[4 * i : 4 * i + 4, :] = hrecv[i]
    rows_all = hfull[...].astype(BF16)[:, :64]
    loads[15].wait()
    loads[16].wait()
    turn = lax.broadcasted_iota(jnp.int32, (8, HD), 1)
    freq = jnp.ones((8, HD), F32)
    for j, value in enumerate(FREQ):
        freq = jnp.where(turn % (HD // 2) == j, float(value), freq)
    angle = pos[my_row].astype(F32) * freq
    cosine = jnp.cos(angle)
    sine = jnp.sin(angle)
    sine = jnp.where(turn < HD // 2, -sine, sine)

    def rotate(value):
        return value * cosine + pltpu.roll(value, HD // 2, 1) * sine

    for copy in swaps:
        copy.wait_recv()

    settle(rb.at[pl.ds(0, 15)], recv_sem.at[2])
    total = jnp.broadcast_to(jnp.sum(rb[...], axis=0), (8, 128))
    bb = pltpu.roll(total, 124, 1)
    ab = pltpu.roll(total, 120, 1)
    similar = ab / jnp.sqrt(total * bb + 1e-06)
    share = 1.0 / jnp.sqrt(2.0 * (1.0 + similar))
    lane8 = lax.broadcasted_iota(jnp.int32, (8, 128), 1)
    shares = [
        share[0:1, m : m + 1] for m in range(4)
    ]

    def merge(init, first, second, factor):
        base = init.astype(F32)
        a = first.astype(F32) - base
        b = second.astype(F32) - base
        return (base + factor * a + factor * b).astype(BF16)

    def merge_into(dst, offset, own, swapped, own_row, other_row, width, factor, step):
        def body(i, _):
            there = pl.ds(pl.multiple_of(i * step, step), step)
            here = pl.ds(pl.multiple_of(c * width + i * step, step), step)
            to = pl.ds(pl.multiple_of(offset + i * step, step), step)
            dst[own_row, to] = merge(own[0, :, here], own[1, :, here], own[2, :, here], factor)
            dst[other_row, to] = merge(
                swapped[0, :, there], swapped[1, :, there], swapped[2, :, there], factor
            )
            return 0

        lax.fori_loop(0, width // step, body, 0, unroll=8 if width > 2560 else 2)

    top, bottom = pl.ds(0, DEPTH), pl.ds(32, DEPTH)
    merge_into(mq, 0, wq, pq, top, bottom, QW // 2, shares[0], 256)

    flat = qsend.reshape(4 * 16 * 8, HD)
    for kind in range(4):
        part = jnp.dot(
            rows_all, mq[:, 1024 * kind : 1024 * (kind + 1)], preferred_element_type=F32
        )
        for j in range(8):
            flat[pl.ds(128 * kind + j, 16, stride=8), :] = part[:, 128 * j : 128 * (j + 1)]

    def piece_for(there):
        return (2 * rem(there, 2) + div(there, 8), slice(None), div(rem(there, 8), 2))

    to_plane(lambda there: qsend.at[piece_for(there)], qrecv.at[xy], 3)
    qrecv[xy] = qsend[my_kind, :, my_row]

    merge_into(mkv, 0, wk, pk, top, bottom, KW // 2, shares[1], 256)
    merge_into(mkv, KW // 2, wv, pv, top, bottom, KW // 2, shares[2], 256)
    new = jnp.dot(rows_all, mkv[...], preferred_element_type=F32)
    flat_new = ksend.reshape(4 * 16 * 2, HD)
    for kind in range(4):
        for j in range(2):
            start = 512 * j + 128 * kind
            flat_new[pl.ds(32 * kind + j, 16, stride=2), :] = new[:, start : start + 128]
    to_plane(lambda there: ksend.at[piece_for(there)], krecv.at[xy], 11)
    krecv[xy] = ksend[my_kind, :, my_row]

    merge_into(
        mo, 0, wo, po, pl.ds(pl.multiple_of(32 * c, 32), 32),
        pl.ds(pl.multiple_of(32 * (1 - c), 32), 32), OW // 2, shares[3], 256,
    )

    def to_z(src, dst, stage):
        for a in LINE[:-1]:
            device = column(a, 0)
            remote(src(device[0]), dst, stage, device).start()

    settle(qrecv.at[pl.ds(0, XY - 1)], recv_sem.at[3])
    zsend[...] = jnp.sum(qrecv[...], axis=0)
    to_z(lambda group: zsend.at[group], zrecv.at[z], 4)
    zrecv[z] = zsend[g]
    send_cache(cv, values, 6, 1 - c, 8, 16)
    settle(krecv.at[pl.ds(0, XY - 1)], recv_sem.at[11])
    nsend[...] = jnp.sum(krecv[...], axis=0)
    to_z(lambda group: nsend.at[group], nrecv.at[z], 12)
    nrecv[z] = nsend[g]

    loads[12].wait()
    loads[13].wait()
    settle(keys.at[pl.ds(0, 31)], recv_sem.at[5])
    settle(values.at[pl.ds(0, 31)], recv_sem.at[6])
    settle(zrecv.at[pl.ds(0, 7)], recv_sem.at[4])
    query = rotate(jnp.sum(zrecv[...], axis=0)).astype(BF16)
    length = lens[my_row]
    lane = lax.broadcasted_iota(jnp.int32, (8, 128), 1)
    low = lane < SPAN
    scores, peaks = [], []
    for chunk in range(8):
        score = lax.dot_general(
            query, keys[4 * chunk : 4 * chunk + 4].reshape(4 * SPAN, HD),
            (((1,), (1,)), ((), ())), preferred_element_type=F32,
        )
        for i in range(2):
            slot = (4 * (2 * chunk + i) + 2 * zh) * SPAN + lane
            valid = slot < length
            part = jnp.where(valid, score[:, 128 * i : 128 * (i + 1)] * SCALE, -1e30)
            left = jnp.max(jnp.where(low, part, -1e30), axis=1, keepdims=True)
            right = jnp.max(jnp.where(low, -1e30, part), axis=1, keepdims=True)
            scores.append((part, valid))
            peaks.append(jnp.where(low, left, right))
    most = peaks[0]
    for peak in peaks[1:]:
        most = jnp.maximum(most, peak)
    most = jnp.maximum(most, pltpu.roll(most, 64, 1))
    mass = jnp.zeros((8, 128), F32)
    mixed = jnp.zeros((24, HD), F32)
    for chunk in range(8):
        terms = []
        for i in range(2):
            (part, valid), peak = scores[2 * chunk + i], peaks[2 * chunk + i]
            weight = jnp.where(valid, jnp.exp(part - peak), 0.0).astype(BF16).astype(F32)
            weight = weight * jnp.exp(peak - most)
            mass = mass + weight
            first = weight.astype(BF16)
            rest = weight - first.astype(F32)
            second = rest.astype(BF16)
            third = (rest - second.astype(F32)).astype(BF16)
            terms.append(jnp.concatenate([first, second, third], axis=0))
        mixed = mixed + jnp.dot(
            jnp.concatenate(terms, axis=1),
            values[4 * chunk : 4 * chunk + 4].reshape(4 * SPAN, HD),
            preferred_element_type=F32,
        )
    mixed = mixed[0:8] + mixed[8:16] + mixed[16:24]
    mass = jnp.sum(mass, axis=1, keepdims=True)
    most = most[:, 0:1]

    settle(nrecv.at[pl.ds(0, 7)], recv_sem.at[12])
    new = jnp.sum(nrecv[...], axis=0)
    new_key = jnp.broadcast_to(new[0:1], (8, HD))
    new_key = rotate(new_key).astype(BF16).astype(F32)
    new_value = new[1:2].astype(BF16).astype(F32)
    own = jnp.sum(query.astype(F32) * new_key, axis=1, keepdims=True) * SCALE
    own = jnp.where(zh == 0, own, most)
    peak = jnp.maximum(most, own)
    old = jnp.exp(most - peak)
    fresh = jnp.where(zh == 0, jnp.exp(own - peak), 0.0)
    mixed = mixed * old + fresh * new_value
    stats = jnp.where(low, peak, mass * old + fresh)
    for j in range(8):
        asend[j, 0:1] = mixed[j : j + 1]
        asend[j, 1:2] = stats[j : j + 1]

    owner = lax.div(my_kv, 2)
    slot = (4 * g + my_row) * 2 + zh

    for a, b, e, k in OWNERS[:-1]:
        j = 4 * rem(x + a, 2) + rem(y + b, 4)
        device = (owner, (div(x, 2) * 8 + j) * 4 + 2 * rem(zh + e, 2) + rem(c + k, 2))
        remote(asend.at[j], arecv.at[slot], 7, device).start()

    @pl.when(owner != g)
    def _():
        remote(asend.at[rem(xy, 8)], arecv.at[slot], 7, (owner, t)).start()
        settle(arecv, recv_sem.at[7])

    @pl.when(owner == g)
    def _():
        arecv[slot] = asend[rem(xy, 8)]
        settle(arecv.at[pl.ds(0, 31)], recv_sem.at[7])

    for i in range(16):
        for side in range(2):
            hd[2 * side, i : i + 1] = arecv[2 * i + side, 0:1]
            hd[2 * side + 1, i : i + 1] = arecv[2 * i + side, 1:2]
    left, right = hd[1], hd[3]
    most = jnp.maximum(left[:, 0:1], right[:, 0:1])
    left_factor = jnp.exp(left[:, 0:1] - most)
    right_factor = jnp.exp(right[:, 0:1] - most)
    heads = (hd[0] * left_factor + hd[2] * right_factor) / (
        left[:, 64:65] * left_factor + right[:, 64:65] * right_factor
    )
    heads = jnp.where(zh == 1, pltpu.roll(heads, 64, 1), heads).astype(BF16)[:, :64]

    for tile in range(20):
        part = jnp.dot(
            heads, mo[:, 128 * tile : 128 * (tile + 1)], preferred_element_type=F32
        )
        for i in range(G):
            others = [4 * a + b for a in range(4) if a != i for b in range(4)]
            if tile >= 8:
                to, at = others[tile - 8], i
            else:
                to, at = 4 * i + tile // 2, (i, 4)[tile % 2]
            bsend[to, at] = part[4 * i : 4 * i + 4]
    to_plane(lambda there: bsend.at[there], brecv.at[xy], 8)
    brecv[xy] = bsend[xy]
    settle(brecv.at[pl.ds(0, XY - 1)], recv_sem.at[8])
    total = jnp.sum(brecv[...], axis=0)
    for i in range(G):
        ysend[i, 0] = total[i]
        ysend[i, 1] = total[4]
    for a in LINE[:-1]:
        device = column(a, 0)
        group = device[0]

        @pl.when(group == x)
        def _():
            remote(ysend.at[group], yrecv.at[z], 9, device).start()

        @pl.when(group != x)
        def _():
            remote(ysend.at[group, 0], yrecv.at[z, 0], 9, device).start()

    yrecv[z] = ysend[g]

    @pl.when(x == g)
    def _():
        settle(yrecv.at[pl.ds(0, 7)], recv_sem.at[9])

    @pl.when(x != g)
    def _():
        settle(yrecv.at[pl.ds(0, 7), 0], recv_sem.at[9])

    osend[:, 0:128] = jnp.sum(yrecv[:, 0], axis=0).astype(BF16)

    def finish(start, tiles):
        src = osend.at[:, pl.ds(0, 128 * tiles)]
        dst = out.at[:, pl.ds(pl.multiple_of(c * (OW // 2) + start, 128), 128 * tiles)]
        for a, b, k in PLANE_CORES[:-1]:
            device = (g, chip(a, b) * 4 + zh * 2 + rem(c + k, 2))
            remote(src, dst, 10, device).start()
        copy = pltpu.make_async_copy(src, dst, load_sem.at[0])
        copy.start()
        copy.wait()
        settle(out.at[:, pl.ds(0, (40 - tiles) * 128)], recv_sem.at[10])

    @pl.when(x == g)
    def _():
        osend[:, 128:256] = jnp.sum(yrecv[:, 1], axis=0).astype(BF16)
        finish(256 * y, 2)

    @pl.when(x < g)
    def _():
        finish(1024 + 128 * xy, 1)

    @pl.when(x > g)
    def _():
        finish(512 + 128 * xy, 1)

    for copy in swaps:
        copy.wait_send()
    for stage, ref, count in (
        (0, hrecv, 3), (1, ra, 15), (2, rb, 15), (3, qrecv, 15), (4, zrecv, 7), (5, keys, 31),
        (6, values, 31), (8, brecv, 15), (11, krecv, 15), (12, nrecv, 7),
    ):
        settle(ref.at[pl.ds(0, count)], send_sem.at[stage])
    settle(out.at[:, pl.ds(0, 31 * 128)], send_sem.at[10])

    @pl.when(x == g)
    def _():
        settle(out.at[:, pl.ds(0, 31 * 128)], send_sem.at[10])

    settle(yrecv.at[pl.ds(0, 7), 0], send_sem.at[9])
    settle(yrecv.at[0, 0], send_sem.at[9])

    @pl.when(x != g)
    def _():
        settle(yrecv.at[0, 0], send_sem.at[9])

    settle(arecv.at[pl.ds(0, 31)], send_sem.at[7])


    @pl.when(owner != g)
    def _():
        settle(arecv.at[0], send_sem.at[7])


def shards(*args):
    hbm = pl.BlockSpec(memory_space=pltpu.HBM)
    f32 = lambda *shape: pltpu.VMEM(shape, F32)
    bf16 = lambda *shape: pltpu.VMEM(shape, BF16)
    return pl.pallas_call(
        kernel,
        out_shape=pltpu.VMEM((R, OW), BF16),
        in_specs=[hbm] * 17,
        out_specs=pl.BlockSpec(memory_space=pl.ANY),
        scratch_shapes=[
            pltpu.SMEM((R,), jnp.int32), pltpu.SMEM((R,), jnp.int32),
            bf16(3, DEPTH, QW), bf16(3, DEPTH, KW), bf16(3, DEPTH, KW), bf16(3, ODEPTH, OW),
            bf16(3, DEPTH, QW // 2), bf16(3, DEPTH, KW // 2), bf16(3, DEPTH, KW // 2), bf16(3, ODEPTH, OW // 2),
            bf16(32, SPAN, HD), bf16(32, SPAN, HD), bf16(R, 5120),
            f32(G, R, HD), f32(G, R, HD), f32(16, HD),
            f32(1, HD), f32(XY, 1, HD), f32(1, HD), f32(16, 1, HD),
            bf16(64, QW // 2), bf16(64, KW), bf16(64, OW // 2),
            f32(4, G, R, 8, HD), f32(XY, G, 8, HD), f32(4, G, R, 2, HD), f32(XY, G, 2, HD),
            f32(G, 8, HD), f32(8, 8, HD), f32(G, 2, HD), f32(8, 2, HD),
            f32(8, 2, HD), f32(32, 2, HD), f32(4, 16, HD),
            f32(XY, 5, R, HD), f32(XY, 5, R, HD), f32(G, 2, R, HD), f32(8, 2, R, HD),
            bf16(R, 2 * HD),
            pltpu.SemaphoreType.DMA((17,)), pltpu.SemaphoreType.DMA((12,)), pltpu.SemaphoreType.DMA((12,)),
            pltpu.SemaphoreType.DMA((13,)), pltpu.SemaphoreType.DMA((13,)),
        ],
        compiler_params=pltpu.CompilerParams(
            collective_id=0, has_side_effects=True, vmem_limit_bytes=24 * 1024 * 1024
        ),
        cost_estimate=pl.CostEstimate(flops=40_000_000, bytes_accessed=4_000_000, transcendentals=100_000),
    )(*(pltpu.with_memory_space_constraint(arg, pltpu.HBM) for arg in args))


def solution(mesh):
    both = P(("group", "tensor"), None)
    cache = P("group", None, "tensor", None)
    in_specs = (both,) * 12 + (P("group", None), cache, cache, P("group"), P("group"))
    return jax.shard_map(
        shards, mesh=mesh, in_specs=in_specs, out_specs=P("group", None), check_vma=False
    )
```
